32 devices in a mesh: tm: 4 (over y, x), space: 8 (over z, core).
Axes of the slice: x: 2, y: 2, z: 4, core: 2. Of those that a mesh axis runs over, the one named last changes fastest.
Arguments:
- frames: bfloat16 [4, 16, 96, 384], P('tm', 'space'), may hold values from -8 to 8
- cache_in: bfloat16 [2, 16, 96, 384], P(None, 'space'), may hold values from -6 to 6
- norm_gain: bfloat16 [384], replicated, may hold values from 0.5 to 1.5
- w_qkv: bfloat16 [384, 1152], replicated, may hold values from -0.5 to 0.5
- b_qkv: bfloat16 [1152], replicated, may hold values from -3 to 3
- w_proj: bfloat16 [384, 384], replicated, may hold values from -1.25 to 1.25
- b_proj: bfloat16 [384], replicated, may hold values from -2 to 2
- w_time: bfloat16 [3, 384, 768], replicated, may hold values from -0.1875 to 0.1875
- b_time: bfloat16 [768], replicated, may hold values from -3 to 3
- w_space: bfloat16 [3, 3, 384, 192], replicated, may hold values from -0.109375 to 0.109375
- b_space: bfloat16 [192], replicated, may hold values from -3 to 3
Outputs:
- decoded: bfloat16 [8, 32, 192, 192], P('tm', 'space')
The draws below stay inside these ranges and needn't reach their ends.
All inputs are finite; a program needn't handle non-finite values.
Results may differ from the reference program's by a relative error of at most 0.01.
Values may be sent and summed in bfloat16 or wider, within the bound.
A program may use at most 64 MiB of HBM per device.

```python
import jax
import jax.numpy as jnp
from jax import lax

C = 384
C2 = 192
COLS = 96
FRAMES = 4
HEIGHT = 16


def draw_frames(key, part):
    shape = (FRAMES, HEIGHT, COLS, C)
    base = jnp.clip(jax.random.normal(jax.random.fold_in(key, 1), shape, jnp.float32), -6.0, 6.0)
    return base.astype(jnp.bfloat16)


def draw_w_qkv(key, part):
    column = jnp.arange(3 * C)
    raw = jax.random.normal(jax.random.fold_in(key, 4), (C, 3 * C), jnp.float32) * C ** (-0.5)
    raw = raw * jnp.where(column < 2 * C, 1.7, 1.0)
    raw = jnp.clip(raw, -0.45, 0.45)
    return raw.astype(jnp.bfloat16)


def levels(key, extent, pieces, smallest, largest):
    loudness = 1.0
    for position, shards_of in pieces:
        draws = jax.random.uniform(jax.random.fold_in(jax.random.fold_in(key, 6), position), (shards_of,), jnp.float32, smallest / len(pieces), largest / len(pieces))
        loudness = loudness * jnp.repeat(jnp.exp(draws), extent[position] // shards_of).reshape((-1,) + (1,) * (len(extent) - 1 - position))
    return loudness


def normal_values(rng, dims, scale, reach, cuts=(), held_as=jnp.bfloat16):
    array = scale * jax.random.normal(rng, dims, jnp.float32)
    if cuts:
        array = array * levels(rng, dims, cuts, -0.22, 0.18)
    return jnp.clip(array, -reach, reach).astype(held_as)


def setup_inputs(seed: int = 0) -> dict:
    key_list = jax.random.split(jax.random.key(seed), 12)
    return {
        "frames": draw_frames(jax.random.fold_in(key_list[11], 71), 0),
        "cache_in": normal_values(key_list[1], (2, HEIGHT, COLS, C), 1.0, 6.0, ((1, 8),)),
        "norm_gain": jnp.clip(1.0 + 0.1 * jax.random.normal(key_list[2], (C,), jnp.float32), 0.5, 1.5).astype(jnp.bfloat16),
        "w_qkv": draw_w_qkv(jax.random.fold_in(key_list[11], 71), 0),
        "b_qkv": normal_values(key_list[4], (3 * C,), 0.5, 3.0),
        "w_proj": normal_values(key_list[5], (C, C), (C // 16) ** -0.5, 1.25),
        "b_proj": normal_values(key_list[6], (C,), 0.3, 2.0),
        "w_time": normal_values(key_list[7], (3, C, 2 * C), (3 * C) ** -0.5, 0.1875),
        "b_time": normal_values(key_list[8], (2 * C,), 0.5, 3.0),
        "w_space": normal_values(key_list[9], (3, 3, C, C2), (9 * C) ** -0.5, 0.109375),
        "b_space": normal_values(key_list[10], (C2,), 0.5, 3.0),
    }


EPSILON = 1e-06

def normalize(frames, norm_gain):
    widened = frames.astype(jnp.float32)
    inverse = lax.rsqrt(lax.optimization_barrier(jnp.mean(widened * widened, axis=-1, keepdims=True)) + EPSILON)
    return (widened * inverse * norm_gain.astype(jnp.float32)).astype(jnp.bfloat16)

def project(rows, weight, bias):
    return (jnp.dot(rows, weight, preferred_element_type=jnp.float32) + bias.astype(jnp.float32)).astype(jnp.bfloat16)

def reference(frames, cache_in, norm_gain, w_qkv, b_qkv, w_proj, b_proj, w_time, b_time, w_space, b_space):
    frame_count, height, width, channels = frames.shape
    normed = normalize(frames, norm_gain).reshape(frame_count, height * width, channels)

    def frame_attention(rows):
        queries = project(rows, w_qkv[:, :channels], b_qkv[:channels])
        key_rows = project(rows, w_qkv[:, channels:2 * channels], b_qkv[channels:2 * channels])
        value_rows = project(rows, w_qkv[:, 2 * channels:], b_qkv[2 * channels:])
        scores = jnp.dot(queries, key_rows.T, preferred_element_type=jnp.float32) * channels ** (-0.5)
        row_max = lax.optimization_barrier(jnp.max(scores, axis=1, keepdims=True))
        weights = jnp.exp(scores - row_max)
        mass = lax.optimization_barrier(jnp.sum(weights, axis=1, keepdims=True))
        return (jnp.dot(weights.astype(jnp.bfloat16), value_rows, preferred_element_type=jnp.float32) / mass).astype(jnp.bfloat16)
    mixed = lax.map(frame_attention, normed).reshape(-1, channels)
    hidden = (frames.reshape(-1, channels).astype(jnp.float32) + jnp.dot(mixed, w_proj, preferred_element_type=jnp.float32) + b_proj.astype(jnp.float32)).astype(jnp.bfloat16)
    hidden = hidden.reshape(frame_count, height * width, channels)
    shifted = jnp.concatenate([cache_in.reshape(2, height * width, channels), hidden], axis=0)
    timed = jnp.zeros((frame_count * height * width, 2 * channels), jnp.float32) + b_time.astype(jnp.float32)
    for offset in range(3):
        timed = timed + jnp.dot(shifted[offset:offset + frame_count].reshape(-1, channels), w_time[offset], preferred_element_type=jnp.float32)
    timed = timed.astype(jnp.bfloat16).reshape(frame_count, height, width, 2 * channels)
    paired = jnp.stack([timed[..., :channels], timed[..., channels:]], axis=1).reshape(2 * frame_count, height, width, channels)

    def spatial(frame):
        upsampled = jnp.repeat(jnp.repeat(frame, 2, axis=0), 2, axis=1)
        padded = jnp.pad(upsampled, ((1, 1), (1, 1), (0, 0)))
        result = jnp.zeros((4 * height * width, w_space.shape[-1]), jnp.float32) + b_space.astype(jnp.float32)
        for row_tap in range(3):
            for col_tap in range(3):
                window = padded[row_tap:row_tap + 2 * height, col_tap:col_tap + 2 * width].reshape(-1, channels)
                result = result + jnp.dot(window, w_space[row_tap, col_tap], preferred_element_type=jnp.float32)
        return result.astype(jnp.bfloat16).reshape(2 * height, 2 * width, w_space.shape[-1])
    return lax.map(spatial, paired)
```

```python
import functools

import jax
import jax.numpy as jnp
from jax import lax
from jax.experimental import pallas as pl
from jax.experimental.pallas import tpu as pltpu
from jax.sharding import PartitionSpec as P

EPSILON = 1e-06
F32 = jnp.float32
BF16 = jnp.bfloat16
MESH = pl.DeviceIdType.MESH


def mm(left, right):
    return jnp.dot(left, right, preferred_element_type=F32)


def mm_t(left, right):
    return lax.dot_general(left, right, (((1,), (1,)), ((), ())), preferred_element_type=F32)


def row_of(ref, start, size):
    return ref[...].astype(F32).reshape(1, -1)[:, start : start + size]


def kernel(
    chips, steps,
    frames, cache, gain, wqkv_h, bqkv, wproj_h, bproj, wtime_h, btime, wspace_h, bspace,
    out_h,
    xg, wqkv, wproj, wtime, wspace, wf, qp, best, mass, total, hid, hist, tacc, tim, halo, abuf,
    wide, outv,
    wsem, grecv, gsend, trecv, tsend, hrecv, hsend, osem,
):
    ch = frames.shape[-1]
    width = frames.shape[2]
    rows = 2 * width
    c2 = wspace.shape[-1]
    t = lax.axis_index("tm")
    s = lax.axis_index("space")
    z, c = s // 2, s % 2
    has_lo, has_hi = z > 0, z < chips - 1
    sib = z * 2 + (1 - c)

    loads = [
        pltpu.make_async_copy(src, dst, wsem.at[i])
        for i, (src, dst) in enumerate(
            ((wqkv_h, wqkv), (wspace_h, wspace), (wproj_h, wproj), (wtime_h, wtime))
        )
    ]
    for load in loads:
        load.start()

    barrier = pltpu.get_barrier_semaphore()
    cross = jnp.where(c == 0, s - 1, s + 1)
    has_cross = jnp.where(c == 0, has_lo, has_hi)
    peers = [
        (has_lo, t, s - 2),
        (has_hi, t, s + 2),
        (has_cross, t, cross),
        (t >= 1, t - 1, s),
        (t >= 2, t - 2, s),
        (t < steps - 1, t + 1, s),
        (t < steps - 2, t + 2, s),
    ]
    pl.semaphore_signal(barrier, inc=1, device_id=(t, sib), device_id_type=MESH)
    greeted = jnp.int32(1)
    for there, pt, ps in peers:
        greeted = greeted + there.astype(jnp.int32)

        @pl.when(there)
        def _(pt=pt, ps=ps):
            pl.semaphore_signal(barrier, inc=1, device_id=(pt, ps), device_id_type=MESH)

    for r in range(2):
        value = frames[0, r].astype(F32)
        inverse = lax.rsqrt(jnp.mean(value * value, axis=-1, keepdims=True) + EPSILON)
        xg[z, c, pl.ds(r * width, width), :] = (value * inverse * row_of(gain, 0, ch)).astype(BF16)

    pl.semaphore_wait(barrier, greeted)

    def block(origin, core, h, kind, target):
        piece = xg.at[origin, core, pl.ds(h * width, width), :]
        return pltpu.make_async_remote_copy(
            src_ref=piece,
            dst_ref=piece,
            send_sem=gsend.at[origin, h, kind],
            recv_sem=grecv.at[origin, core, h],
            device_id=(t, target),
            device_id_type=MESH,
        )

    for h in range(2):
        @pl.when(has_hi)
        def _(h=h):
            block(z, c, h, 0, s + 2).start()

        @pl.when(has_lo)
        def _(h=h):
            block(z, c, h, 2, s - 2).start()

        block(z, c, h, 1, sib).start()

    loads[0].wait()
    mine = xg[z, c]
    queries = (mm(mine, wqkv[:, :ch]) + row_of(bqkv, 0, ch)).astype(BF16)
    scale = ch ** (-0.5)
    qp[...] = (mm_t(queries, wqkv[:, ch : 2 * ch]) * scale).astype(BF16)
    offset = jnp.sum(queries.astype(F32) * row_of(bqkv, ch, ch), axis=1, keepdims=True) * scale

    def scores_of(origin):
        keys = xg[origin].reshape(2 * rows, ch)
        return keys, mm_t(qp[...], keys) + offset

    loads[1].wait()
    groups = (((0,), (1, 2)), ((0, 1), (2,)))
    for pr in range(2):
        for pc in range(2):
            for dr in range(2):
                for dc in range(2):
                    part = None
                    for i in groups[pr][dr]:
                        for j in groups[pc][dc]:
                            tap = wspace[i, j].astype(F32)
                            part = tap if part is None else part + tap
                    at = pl.ds((2 * dr + dc) * ch, ch)
                    wf[pr, pc, at, :] = jnp.concatenate(
                        [part, jnp.zeros((ch, 256 - c2), F32)], axis=1
                    ).astype(BF16)

    for h in range(2):
        block(z, 1 - c, h, 1, sib).wait_recv()
    keys, scores = scores_of(z)
    top = jnp.max(scores, axis=1, keepdims=True)
    weights = jnp.exp(scores - top)
    best[...] = top
    mass[...] = jnp.sum(weights, axis=1, keepdims=True)
    total[...] = mm(weights.astype(BF16), keys)

    def absorb(origin):
        keys, scores = scores_of(origin)
        top = jnp.maximum(best[...], jnp.max(scores, axis=1, keepdims=True))
        weights = jnp.exp(scores - top)
        shrink = jnp.exp(best[...] - top)
        best[...] = top
        mass[...] = mass[...] * shrink + jnp.sum(weights, axis=1, keepdims=True)
        total[...] = total[...] * shrink + mm(weights.astype(BF16), keys)

    @pl.loop(1, chips)
    def _(d):
        sides = (
            (z - d, z - d >= 0, has_hi, s + 2),
            (z + d, z + d <= chips - 1, has_lo, s - 2),
        )
        for h in range(2):
            for origin, there, onward, target in sides:
                @pl.when(there)
                def _(origin=origin, onward=onward, target=target, h=h):
                    block(origin, c, h, 1, sib).wait_recv()

                    @pl.when(onward)
                    def _():
                        block(origin, c, h, 0, target).start()

                    block(origin, c, h, 1, sib).start()

        for origin, there, onward, target in sides:
            @pl.when(there)
            def _(origin=origin):
                for h in range(2):
                    block(origin, 1 - c, h, 1, sib).wait_recv()
                absorb(origin)

    loads[2].wait()

    def passed(h, kind, target):
        return pltpu.make_async_remote_copy(
            src_ref=hid.at[h],
            dst_ref=hist.at[kind, h],
            send_sem=tsend.at[kind, h],
            recv_sem=trecv.at[kind, h],
            device_id=(target, s),
            device_id_type=MESH,
        )

    for h in range(2):
        at = pl.ds(h * width, width)
        rows_mixed = (total[at, :] / mass[at, :]).astype(BF16)
        mixed = (mm(rows_mixed, wqkv[:, 2 * ch :]) + row_of(bqkv, 2 * ch, ch)).astype(BF16)
        hid[h] = (
            frames[0, h].astype(F32) + mm(mixed, wproj[...]) + row_of(bproj, 0, ch)
        ).astype(BF16)

        @pl.when(t < steps - 1)
        def _(h=h):
            passed(h, 1, t + 1).start()

        @pl.when(t < steps - 2)
        def _(h=h):
            passed(h, 0, t + 2).start()

    @pl.when(t == 0)
    def _():
        hist[0] = cache[0]
        hist[1] = cache[1]

    @pl.when(t == 1)
    def _():
        hist[0] = cache[1]

    loads[3].wait()
    tacc[...] = mm(hid[...].reshape(rows, ch), wtime[2]) + row_of(btime, 0, 2 * ch)

    first = lax.broadcasted_iota(jnp.int32, (width, ch), 0) == 0
    final = lax.broadcasted_iota(jnp.int32, (width, ch), 0) == width - 1

    def spread(index, row):
        for f in range(2):
            value = row[:, f * ch : (f + 1) * ch]
            wider = value.astype(F32)
            abuf[index, f, :, :ch] = jnp.where(first, 0.0, pltpu.roll(wider, 1, 0)).astype(BF16)
            abuf[index, f, :, ch : 2 * ch] = value
            abuf[index, f, :, 2 * ch :] = jnp.where(
                final, 0.0, pltpu.roll(wider, width - 1, 0)
            ).astype(BF16)

    n_space = 2 * chips

    def edge(r, target):
        return pltpu.make_async_remote_copy(
            src_ref=tim.at[r],
            dst_ref=halo.at[1 - r],
            send_sem=hsend.at[r],
            recv_sem=hrecv.at[1 - r],
            device_id=(t, target),
            device_id_type=MESH,
        )

    for r in range(2):
        @pl.when(t >= 1)
        def _(r=r):
            passed(r, 1, t - 1).wait_recv()

        @pl.when(t >= 2)
        def _(r=r):
            passed(r, 0, t - 2).wait_recv()

        row = (
            tacc[pl.ds(r * width, width), :] + mm(hist[1, r], wtime[1]) + mm(hist[0, r], wtime[0])
        ).astype(BF16)
        tim[r] = row
        goes = (s > 0) if r == 0 else (s < n_space - 1)

        @pl.when(goes)
        def _(r=r):
            edge(r, s - 1 if r == 0 else s + 1).start()

        spread(1 + r, row)

    def convolve(j):
        upper, pr = ((0, 0), (1, 1), (1, 0), (2, 1))[j]
        for pc in range(2):
            value = jnp.concatenate([row_of(bspace, 0, c2), jnp.zeros((1, 256 - c2), F32)], axis=1)
            for dr in range(2):
                lhs = abuf[upper + dr, :, :, pc * ch : (pc + 2) * ch].reshape(rows, 2 * ch)
                value = value + mm(lhs, wf[pr, pc, 2 * dr * ch : 2 * (dr + 1) * ch, :])
            for half in range(2):
                for f in range(2):
                    wide[half, f, pl.ds(pc, width, stride=2), :] = value[
                        f * width : (f + 1) * width, half * 128 : (half + 1) * 128
                    ]
        for f in range(2):
            outv[j, f, :, :128] = wide[0, f].astype(BF16)
            outv[j, f, :, 128:] = wide[1, f, :, : c2 - 128].astype(BF16)

    def give(j):
        return pltpu.make_async_copy(outv.at[j], out_h.at[:, j], osem.at[j])

    for j in (1, 2):
        convolve(j)
        give(j).start()

    for side in range(2):
        comes = (s > 0) if side == 0 else (s < n_space - 1)

        @pl.when(comes)
        def _(side=side):
            edge(1 - side, s - 1 if side == 0 else s + 1).wait_recv()

        @pl.when(jnp.logical_not(comes))
        def _(side=side):
            halo[side] = jnp.zeros(halo.shape[1:], BF16)

        spread(3 * side, halo[side])
        convolve(3 * side)
        give(3 * side).start()

    for h in range(2):
        @pl.when(has_hi)
        def _(h=h):
            block(z, c, h, 0, s + 2).wait_send()

        @pl.when(has_lo)
        def _(h=h):
            block(z, c, h, 2, s - 2).wait_send()

        block(z, c, h, 1, sib).wait_send()

    @pl.loop(1, chips)
    def _(d):
        for h in range(2):
            for origin, there, onward, target in (
                (z - d, z - d >= 0, has_hi, s + 2),
                (z + d, z + d <= chips - 1, has_lo, s - 2),
            ):
                @pl.when(there)
                def _(origin=origin, onward=onward, target=target, h=h):
                    @pl.when(onward)
                    def _():
                        block(origin, c, h, 0, target).wait_send()

                    block(origin, c, h, 1, sib).wait_send()

    for h in range(2):
        @pl.when(t < steps - 1)
        def _(h=h):
            passed(h, 1, t + 1).wait_send()

        @pl.when(t < steps - 2)
        def _(h=h):
            passed(h, 0, t + 2).wait_send()

    @pl.when(s > 0)
    def _():
        edge(0, s - 1).wait_send()

    @pl.when(s < n_space - 1)
    def _():
        edge(1, s + 1).wait_send()

    for j in range(4):
        give(j).wait()


def solution(mesh):
    chips, steps = mesh.shape["space"] // 2, mesh.shape["tm"]

    def body(frames, cache, gain, wqkv, bqkv, wproj, bproj, wtime, btime, wspace, bspace):
        _, _, width, ch = frames.shape
        c2 = wspace.shape[-1]
        cache = cache.reshape((2,) + frames.shape[1:])
        rows = 2 * width
        vmem = pl.BlockSpec(memory_space=pltpu.VMEM)
        away = pl.BlockSpec(memory_space=pl.ANY)
        dma = pltpu.SemaphoreType.DMA
        return pl.pallas_call(
            functools.partial(kernel, chips, steps),
            out_shape=jax.ShapeDtypeStruct((2, 4, 2 * width, c2), BF16),
            in_specs=[vmem, vmem, vmem, away, vmem, away, vmem, away, vmem, away, vmem],
            out_specs=away,
            scratch_shapes=[
                pltpu.VMEM((chips, 2, rows, ch), BF16),
                pltpu.VMEM(wqkv.shape, BF16),
                pltpu.VMEM(wproj.shape, BF16),
                pltpu.VMEM(wtime.shape, BF16),
                pltpu.VMEM(wspace.shape, BF16),
                pltpu.VMEM((2, 2, 4 * ch, 256), BF16),
                pltpu.VMEM((rows, ch), BF16),
                pltpu.VMEM((rows, 1), F32),
                pltpu.VMEM((rows, 1), F32),
                pltpu.VMEM((rows, ch), F32),
                pltpu.VMEM((2, width, ch), BF16),
                pltpu.VMEM((2, 2, width, ch), BF16),
                pltpu.VMEM((rows, 2 * ch), F32),
                pltpu.VMEM((2, width, 2 * ch), BF16),
                pltpu.VMEM((2, width, 2 * ch), BF16),
                pltpu.VMEM((4, 2, width, 3 * ch), BF16),
                pltpu.VMEM((2, 2, 2 * width, 128), F32),
                pltpu.VMEM((4, 2, 2 * width, c2), BF16),
                dma((4,)),
                dma((chips, 2, 2)),
                dma((chips, 2, 3)),
                dma((2, 2)),
                dma((2, 2)),
                dma((2,)),
                dma((2,)),
                dma((4,)),
            ],
            compiler_params=pltpu.CompilerParams(
                collective_id=0, has_side_effects=True, vmem_limit_bytes=56 * 2**20
            ),
            cost_estimate=pl.CostEstimate(
                flops=2 * 10**9, bytes_accessed=6 * 10**6, transcendentals=300000
            ),
        )(frames, cache, gain, wqkv, bqkv, wproj, bproj, wtime, btime, wspace, bspace)

    return jax.shard_map(
        body,
        mesh=mesh,
        in_specs=(P("tm", "space", None, None), P(None, "space", None, None)) + (P(),) * 9,
        out_specs=P("tm", "space", None, None),
        check_vma=False,
    )
```

```python
import functools

import jax
import jax.numpy as jnp
from jax import lax
from jax.experimental import pallas as pl
from jax.experimental.pallas import tpu as pltpu
from jax.sharding import PartitionSpec as P

EPSILON = 1e-06
F32 = jnp.float32
BF16 = jnp.bfloat16
MESH = pl.DeviceIdType.MESH


def mm(left, right):
    return jnp.dot(left, right, preferred_element_type=F32)


def mm_t(left, right):
    return lax.dot_general(left, right, (((1,), (1,)), ((), ())), preferred_element_type=F32)


def row_of(ref, start, size):
    return ref[...].astype(F32).reshape(1, -1)[:, start : start + size]


def kernel(
    chips, steps,
    frames, cache, gain, wqkv_h, bqkv, wproj_h, bproj, wtime_h, btime, wspace_h, bspace,
    out_h,
    xg, wqkv, wproj, wtime, wspace, wf, qp, best, mass, total, hid, hist, tacc, tim, halo, abuf,
    wide, outv,
    wsem, grecv, gsend, trecv, tsend, hrecv, hsend, osem,
):
    ch = frames.shape[-1]
    width = frames.shape[2]
    rows = 2 * width
    c2 = wspace.shape[2]
    relay = steps == 4
    t = lax.axis_index("tm")
    s = lax.axis_index("space")
    z, c = s // 2, s % 2
    has_lo, has_hi = z > 0, z < chips - 1
    sib = z * 2 + (1 - c)

    loads = [
        pltpu.make_async_copy(src, dst, wsem.at[i])
        for i, (src, dst) in enumerate(
            ((wqkv_h, wqkv), (wspace_h, wspace), (wproj_h, wproj), (wtime_h, wtime))
        )
    ]
    for load in loads:
        load.start()

    barrier = pltpu.get_barrier_semaphore()
    cross = jnp.where(c == 0, s - 1, s + 1)
    has_cross = jnp.where(c == 0, has_lo, has_hi)
    peers = [
        (has_lo, t, s - 2),
        (has_hi, t, s + 2),
        (has_cross, t, cross),
        (t >= 1, t - 1, s),
        (t >= 2, t - 2, s),
        (t < steps - 1, t + 1, s),
        (t < steps - 2, t + 2, s),
    ]
    pl.semaphore_signal(barrier, inc=1, device_id=(t, sib), device_id_type=MESH)
    greeted = jnp.int32(1)
    for there, pt, ps in peers:
        greeted = greeted + there.astype(jnp.int32)

        @pl.when(there)
        def _(pt=pt, ps=ps):
            pl.semaphore_signal(barrier, inc=1, device_id=(pt, ps), device_id_type=MESH)

    for r in range(2):
        value = frames[0, r].astype(F32)
        inverse = lax.rsqrt(jnp.mean(value * value, axis=-1, keepdims=True) + EPSILON)
        xg[z, c, pl.ds(r * width, width), :] = (value * inverse * row_of(gain, 0, ch)).astype(BF16)

    pl.semaphore_wait(barrier, greeted)

    def block(origin, core, h, kind, target):
        piece = xg.at[origin, core, pl.ds(h * width, width), :]
        return pltpu.make_async_remote_copy(
            src_ref=piece,
            dst_ref=piece,
            send_sem=gsend.at[origin, h, kind],
            recv_sem=grecv.at[origin, core, h],
            device_id=(t, target),
            device_id_type=MESH,
        )

    for h in range(2):
        @pl.when(has_hi)
        def _(h=h):
            block(z, c, h, 0, s + 2).start()

        @pl.when(has_lo)
        def _(h=h):
            block(z, c, h, 2, s - 2).start()

        block(z, c, h, 1, sib).start()

    loads[0].wait()
    mine = xg[z, c]
    queries = (mm(mine, wqkv[:, :ch]) + row_of(bqkv, 0, ch)).astype(BF16)
    scale = ch ** (-0.5)
    qp[...] = (mm_t(queries, wqkv[:, ch : 2 * ch]) * scale).astype(BF16)
    offset = jnp.sum(queries.astype(F32) * row_of(bqkv, ch, ch), axis=1, keepdims=True) * scale

    def scores_of(origin):
        keys = xg[origin].reshape(2 * rows, ch)
        return keys, mm_t(qp[...], keys) + offset

    for h in range(2):
        block(z, 1 - c, h, 1, sib).wait_recv()
    keys, scores = scores_of(z)
    top = jnp.max(scores, axis=1, keepdims=True)
    weights = jnp.exp(scores - top)
    best[...] = top
    mass[...] = jnp.sum(weights, axis=1, keepdims=True)
    total[...] = mm(weights.astype(BF16), keys)

    def absorb(origin):
        keys, scores = scores_of(origin)
        top = jnp.maximum(best[...], jnp.max(scores, axis=1, keepdims=True))
        weights = jnp.exp(scores - top)
        shrink = jnp.exp(best[...] - top)
        best[...] = top
        mass[...] = mass[...] * shrink + jnp.sum(weights, axis=1, keepdims=True)
        total[...] = total[...] * shrink + mm(weights.astype(BF16), keys)

    def sides_of(d):
        return (
            (z - d, z - d >= 0, has_hi, s + 2),
            (z + d, z + d <= chips - 1, has_lo, s - 2),
        )

    def forward(d):
        for h in range(2):
            for origin, there, onward, target in sides_of(d):
                @pl.when(there)
                def _(origin=origin, onward=onward, target=target, h=h):
                    block(origin, c, h, 1, sib).wait_recv()

                    @pl.when(onward)
                    def _():
                        block(origin, c, h, 0, target).start()

                    block(origin, c, h, 1, sib).start()

    def take(d):
        for origin, there, onward, target in sides_of(d):
            @pl.when(there)
            def _(origin=origin):
                for h in range(2):
                    block(origin, 1 - c, h, 1, sib).wait_recv()
                absorb(origin)

    forward(1)

    loads[1].wait()
    groups = (((0,), (1, 2)), ((0, 1), (2,)))
    for pr in range(2):
        for pc in range(2):
            for dr in range(2):
                for dc in range(2):
                    part = None
                    for i in groups[pr][dr]:
                        for j in groups[pc][dc]:
                            tap = wspace[i, j].astype(F32)
                            part = tap if part is None else part + tap
                    at = (2 * dr + dc) * ch
                    wf[pr, pc, :c2, at : at + ch] = part.astype(BF16)
            wf[pr, pc, c2:, :] = jnp.zeros((256 - c2, 4 * ch), BF16)

    take(1)

    @pl.loop(2, chips)
    def _(d):
        forward(d)
        take(d)

    loads[2].wait()

    def passed(h, kind, target):
        return pltpu.make_async_remote_copy(
            src_ref=hid.at[h],
            dst_ref=hist.at[kind, h],
            send_sem=tsend.at[kind, h],
            recv_sem=trecv.at[kind, h],
            device_id=(target, s),
            device_id_type=MESH,
        )

    def relayed(h):
        return pltpu.make_async_remote_copy(
            src_ref=hist.at[0, h],
            dst_ref=hist.at[1, h],
            send_sem=tsend.at[1, h],
            recv_sem=trecv.at[1, h],
            device_id=(t - 1, s),
            device_id_type=MESH,
        )

    sends_near = (t == 0) | (t == 2) if relay else t < steps - 1

    for h in range(2):
        at = pl.ds(h * width, width)
        rows_mixed = (total[at, :] / mass[at, :]).astype(BF16)
        mixed = (mm(rows_mixed, wqkv[:, 2 * ch :]) + row_of(bqkv, 2 * ch, ch)).astype(BF16)
        hid[h] = (
            frames[0, h].astype(F32) + mm(mixed, wproj[...]) + row_of(bproj, 0, ch)
        ).astype(BF16)

        @pl.when(sends_near)
        def _(h=h):
            passed(h, 1, t + 1).start()

        @pl.when(t < steps - 2)
        def _(h=h):
            passed(h, 0, t + 2).start()

    @pl.when(t == 0)
    def _():
        hist[0] = cache[0]
        hist[1] = cache[1]

    @pl.when(t == 1)
    def _():
        hist[0] = cache[1]

    loads[3].wait()
    tacc[...] = mm(hid[...].reshape(rows, ch), wtime[2]) + row_of(btime, 0, 2 * ch)

    first = lax.broadcasted_iota(jnp.int32, (width, ch), 0) == 0
    final = lax.broadcasted_iota(jnp.int32, (width, ch), 0) == width - 1

    def spread(index, row):
        for f in range(2):
            value = row[:, f * ch : (f + 1) * ch]
            wider = value.astype(F32)
            abuf[index, f, :, :ch] = jnp.where(first, 0.0, pltpu.roll(wider, 1, 0)).astype(BF16)
            abuf[index, f, :, ch : 2 * ch] = value
            abuf[index, f, :, 2 * ch :] = jnp.where(
                final, 0.0, pltpu.roll(wider, width - 1, 0)
            ).astype(BF16)

    n_space = 2 * chips

    def edge(r, target):
        return pltpu.make_async_remote_copy(
            src_ref=tim.at[r],
            dst_ref=halo.at[1 - r],
            send_sem=hsend.at[r],
            recv_sem=hrecv.at[1 - r],
            device_id=(t, target),
            device_id_type=MESH,
        )

    for r in range(2):
        @pl.when(t >= 2)
        def _(r=r):
            passed(r, 0, t - 2).wait_recv()

        if relay:
            @pl.when(t == 3)
            def _(r=r):
                relayed(r).start()

        @pl.when(t >= 1)
        def _(r=r):
            passed(r, 1, t - 1).wait_recv()

        row = (
            tacc[pl.ds(r * width, width), :] + mm(hist[1, r], wtime[1]) + mm(hist[0, r], wtime[0])
        ).astype(BF16)
        tim[r] = row
        goes = (s > 0) if r == 0 else (s < n_space - 1)

        @pl.when(goes)
        def _(r=r):
            edge(r, s - 1 if r == 0 else s + 1).start()

        spread(1 + r, row)

    def convolve(j):
        upper, pr = ((0, 0), (1, 1), (1, 0), (2, 1))[j]
        for pc in range(2):
            value = jnp.concatenate([row_of(bspace, 0, c2), jnp.zeros((1, 256 - c2), F32)], axis=1)
            for dr in range(2):
                lhs = abuf[upper + dr, :, :, pc * ch : (pc + 2) * ch].reshape(rows, 2 * ch)
                value = value + mm_t(lhs, wf[pr, pc, :, 2 * dr * ch : 2 * (dr + 1) * ch])
            for half in range(2):
                for f in range(2):
                    wide[half, f, pl.ds(pc, width, stride=2), :] = value[
                        f * width : (f + 1) * width, half * 128 : (half + 1) * 128
                    ]
        for f in range(2):
            outv[j, f, :, :128] = wide[0, f].astype(BF16)
            outv[j, f, :, 128:] = wide[1, f, :, : c2 - 128].astype(BF16)

    def give(j):
        return pltpu.make_async_copy(outv.at[j], out_h.at[:, j], osem.at[j])

    for j in (1, 2):
        convolve(j)
        give(j).start()

    for side in range(2):
        comes = (s > 0) if side == 0 else (s < n_space - 1)

        @pl.when(comes)
        def _(side=side):
            edge(1 - side, s - 1 if side == 0 else s + 1).wait_recv()

        @pl.when(jnp.logical_not(comes))
        def _(side=side):
            halo[side] = jnp.zeros(halo.shape[1:], BF16)

        spread(3 * side, halo[side])
        convolve(3 * side)
        give(3 * side).start()

    for h in range(2):
        @pl.when(has_hi)
        def _(h=h):
            block(z, c, h, 0, s + 2).wait_send()

        @pl.when(has_lo)
        def _(h=h):
            block(z, c, h, 2, s - 2).wait_send()

        block(z, c, h, 1, sib).wait_send()

    @pl.loop(1, chips)
    def _(d):
        for h in range(2):
            for origin, there, onward, target in (
                (z - d, z - d >= 0, has_hi, s + 2),
                (z + d, z + d <= chips - 1, has_lo, s - 2),
            ):
                @pl.when(there)
                def _(origin=origin, onward=onward, target=target, h=h):
                    @pl.when(onward)
                    def _():
                        block(origin, c, h, 0, target).wait_send()

                    block(origin, c, h, 1, sib).wait_send()

    for h in range(2):
        @pl.when(sends_near)
        def _(h=h):
            passed(h, 1, t + 1).wait_send()

        @pl.when(t < steps - 2)
        def _(h=h):
            passed(h, 0, t + 2).wait_send()

    if relay:
        @pl.when(t == 3)
        def _():
            for h in range(2):
                relayed(h).wait_send()

    @pl.when(s > 0)
    def _():
        edge(0, s - 1).wait_send()

    @pl.when(s < n_space - 1)
    def _():
        edge(1, s + 1).wait_send()

    for j in range(4):
        give(j).wait()


def solution(mesh):
    chips, steps = mesh.shape["space"] // 2, mesh.shape["tm"]

    def body(frames, cache, gain, wqkv, bqkv, wproj, bproj, wtime, btime, wspace, bspace):
        _, _, width, ch = frames.shape
        c2 = wspace.shape[-1]
        wspace = jnp.swapaxes(wspace, 2, 3)
        cache = cache.reshape((2,) + frames.shape[1:])
        rows = 2 * width
        vmem = pl.BlockSpec(memory_space=pltpu.VMEM)
        away = pl.BlockSpec(memory_space=pl.ANY)
        dma = pltpu.SemaphoreType.DMA
        return pl.pallas_call(
            functools.partial(kernel, chips, steps),
            out_shape=jax.ShapeDtypeStruct((2, 4, 2 * width, c2), BF16),
            in_specs=[vmem, vmem, vmem, away, vmem, away, vmem, away, vmem, away, vmem],
            out_specs=away,
            scratch_shapes=[
                pltpu.VMEM((chips, 2, rows, ch), BF16),
                pltpu.VMEM(wqkv.shape, BF16),
                pltpu.VMEM(wproj.shape, BF16),
                pltpu.VMEM(wtime.shape, BF16),
                pltpu.VMEM(wspace.shape, BF16),
                pltpu.VMEM((2, 2, 256, 4 * ch), BF16),
                pltpu.VMEM((rows, ch), BF16),
                pltpu.VMEM((rows, 1), F32),
                pltpu.VMEM((rows, 1), F32),
                pltpu.VMEM((rows, ch), F32),
                pltpu.VMEM((2, width, ch), BF16),
                pltpu.VMEM((2, 2, width, ch), BF16),
                pltpu.VMEM((rows, 2 * ch), F32),
                pltpu.VMEM((2, width, 2 * ch), BF16),
                pltpu.VMEM((2, width, 2 * ch), BF16),
                pltpu.VMEM((4, 2, width, 3 * ch), BF16),
                pltpu.VMEM((2, 2, 2 * width, 128), F32),
                pltpu.VMEM((4, 2, 2 * width, c2), BF16),
                dma((4,)),
                dma((chips, 2, 2)),
                dma((chips, 2, 3)),
                dma((2, 2)),
                dma((2, 2)),
                dma((2,)),
                dma((2,)),
                dma((4,)),
            ],
            compiler_params=pltpu.CompilerParams(
                collective_id=0, has_side_effects=True, vmem_limit_bytes=56 * 2**20
            ),
            cost_estimate=pl.CostEstimate(
                flops=2 * 10**9, bytes_accessed=6 * 10**6, transcendentals=300000
            ),
        )(frames, cache, gain, wqkv, bqkv, wproj, bproj, wtime, btime, wspace, bspace)

    return jax.shard_map(
        body,
        mesh=mesh,
        in_specs=(P("tm", "space", None, None), P(None, "space", None, None)) + (P(),) * 9,
        out_specs=P("tm", "space", None, None),
        check_vma=False,
    )
```

```python
import functools

import jax
import jax.numpy as jnp
from jax import lax
from jax.experimental import pallas as pl
from jax.experimental.pallas import tpu as pltpu
from jax.sharding import PartitionSpec as P

EPSILON = 1e-06
F32 = jnp.float32
BF16 = jnp.bfloat16
MESH = pl.DeviceIdType.MESH


def mm(left, right):
    return jnp.dot(left, right, preferred_element_type=F32)


def mm_t(left, right):
    return lax.dot_general(left, right, (((1,), (1,)), ((), ())), preferred_element_type=F32)


def row_of(ref, start, size):
    return ref[...].astype(F32).reshape(1, -1)[:, start : start + size]


def kernel(
    chips, steps,
    frames, cache, gain, wqkv_h, bqkv, wproj_h, bproj, wtime_h, btime, wspace_h, bspace,
    out_h,
    xg, wqkv, wproj, wtime, wspace, wf, qp, best, mass, total, hid, hist, tacc, tim, halo, abuf,
    wide, outv,
    wsem, grecv, gsend, trecv, tsend, hrecv, hsend, osem, csem,
):
    ch = frames.shape[-1]
    width = frames.shape[2]
    rows = 2 * width
    c2 = wspace.shape[2]
    t = lax.axis_index("tm")
    s = lax.axis_index("space")
    z, c = s // 2, s % 2
    has_lo, has_hi = z > 0, z < chips - 1
    sib = z * 2 + (1 - c)

    loads = [
        pltpu.make_async_copy(src, dst, wsem.at[i])
        for i, (src, dst) in enumerate(
            ((wqkv_h, wqkv), (wspace_h, wspace), (wproj_h, wproj), (wtime_h, wtime))
        )
    ]
    for load in loads:
        load.start()

    def cached(source, slot):
        return pltpu.make_async_copy(cache.at[source], hist.at[slot], csem.at[slot])

    @pl.when(t == 0)
    def _():
        cached(0, 0).start()
        cached(1, 1).start()

    @pl.when(t == 1)
    def _():
        cached(1, 0).start()

    barrier = pltpu.get_barrier_semaphore()
    cross = jnp.where(c == 0, s - 1, s + 1)
    has_cross = jnp.where(c == 0, has_lo, has_hi)
    peers = [
        (has_lo, t, s - 2),
        (has_hi, t, s + 2),
        (has_cross, t, cross),
        (t >= 1, t - 1, s),
        (t >= 2, t - 2, s),
        (t < steps - 1, t + 1, s),
        (t < steps - 2, t + 2, s),
    ]
    pl.semaphore_signal(barrier, inc=1, device_id=(t, sib), device_id_type=MESH)
    greeted = jnp.int32(1)
    for there, pt, ps in peers:
        greeted = greeted + there.astype(jnp.int32)

        @pl.when(there)
        def _(pt=pt, ps=ps):
            pl.semaphore_signal(barrier, inc=1, device_id=(pt, ps), device_id_type=MESH)

    for r in range(2):
        value = frames[0, r].astype(F32)
        inverse = lax.rsqrt(jnp.mean(value * value, axis=-1, keepdims=True) + EPSILON)
        xg[z, c, pl.ds(r * width, width), :] = (value * inverse * row_of(gain, 0, ch)).astype(BF16)

    pl.semaphore_wait(barrier, greeted)

    def block(origin, core, h, kind, target):
        piece = xg.at[origin, core, pl.ds(h * width, width), :]
        return pltpu.make_async_remote_copy(
            src_ref=piece,
            dst_ref=piece,
            send_sem=gsend.at[origin, h, kind],
            recv_sem=grecv.at[origin, core, h],
            device_id=(t, target),
            device_id_type=MESH,
        )

    for h in range(2):
        @pl.when(has_hi)
        def _(h=h):
            block(z, c, h, 0, s + 2).start()

        @pl.when(has_lo)
        def _(h=h):
            block(z, c, h, 2, s - 2).start()

        block(z, c, h, 1, sib).start()

    loads[0].wait()
    mine = xg[z, c]
    queries = (mm(mine, wqkv[:, :ch]) + row_of(bqkv, 0, ch)).astype(BF16)
    scale = ch ** (-0.5)
    qp[...] = (mm_t(queries, wqkv[:, ch : 2 * ch]) * scale).astype(BF16)
    offset = jnp.sum(queries.astype(F32) * row_of(bqkv, ch, ch), axis=1, keepdims=True) * scale

    def scores_of(origin):
        keys = xg[origin].reshape(2 * rows, ch)
        return keys, mm_t(qp[...], keys) + offset

    for h in range(2):
        block(z, 1 - c, h, 1, sib).wait_recv()
    keys, scores = scores_of(z)
    top = jnp.max(scores, axis=1, keepdims=True)
    weights = jnp.exp(scores - top)
    best[...] = top
    mass[...] = jnp.sum(weights, axis=1, keepdims=True)
    total[...] = mm(weights.astype(BF16), keys)

    def absorb(origin):
        keys, scores = scores_of(origin)
        top = jnp.maximum(best[...], jnp.max(scores, axis=1, keepdims=True))
        weights = jnp.exp(scores - top)
        shrink = jnp.exp(best[...] - top)
        best[...] = top
        mass[...] = mass[...] * shrink + jnp.sum(weights, axis=1, keepdims=True)
        total[...] = total[...] * shrink + mm(weights.astype(BF16), keys)

    def sides_of(d):
        return (
            (z - d, z - d >= 0, has_hi, s + 2),
            (z + d, z + d <= chips - 1, has_lo, s - 2),
        )

    def forward(d):
        for h in range(2):
            for origin, there, onward, target in sides_of(d):
                @pl.when(there)
                def _(origin=origin, onward=onward, target=target, h=h):
                    block(origin, c, h, 1, sib).wait_recv()

                    @pl.when(onward)
                    def _():
                        block(origin, c, h, 0, target).start()

                    block(origin, c, h, 1, sib).start()

    def take(d):
        for origin, there, onward, target in sides_of(d):
            @pl.when(there)
            def _(origin=origin):
                for h in range(2):
                    block(origin, 1 - c, h, 1, sib).wait_recv()
                absorb(origin)

    forward(1)

    loads[1].wait()
    groups = (((0,), (1, 2)), ((0, 1), (2,)))
    for pr in range(2):
        for pc in range(2):
            for dr in range(2):
                for dc in range(2):
                    part = None
                    for i in groups[pr][dr]:
                        for j in groups[pc][dc]:
                            tap = wspace[i, j].astype(F32)
                            part = tap if part is None else part + tap
                    at = (2 * dr + dc) * ch
                    wf[pr, pc, :c2, at : at + ch] = part.astype(BF16)
            wf[pr, pc, c2:, :] = jnp.zeros((256 - c2, 4 * ch), BF16)

    take(1)

    @pl.loop(2, chips)
    def _(d):
        forward(d)
        take(d)

    loads[2].wait()

    def passed(h, kind, target):
        return pltpu.make_async_remote_copy(
            src_ref=hid.at[h],
            dst_ref=hist.at[kind, h],
            send_sem=tsend.at[kind, h],
            recv_sem=trecv.at[kind, h],
            device_id=(target, s),
            device_id_type=MESH,
        )

    for h in range(2):
        at = pl.ds(h * width, width)
        rows_mixed = (total[at, :] / mass[at, :]).astype(BF16)
        mixed = (mm(rows_mixed, wqkv[:, 2 * ch :]) + row_of(bqkv, 2 * ch, ch)).astype(BF16)
        hid[h] = (
            frames[0, h].astype(F32) + mm(mixed, wproj[...]) + row_of(bproj, 0, ch)
        ).astype(BF16)

        @pl.when(t < steps - 1)
        def _(h=h):
            passed(h, 1, t + 1).start()

        @pl.when(t < steps - 2)
        def _(h=h):
            passed(h, 0, t + 2).start()

    @pl.when(t == 0)
    def _():
        cached(0, 0).wait()
        cached(1, 1).wait()

    @pl.when(t == 1)
    def _():
        cached(1, 0).wait()

    loads[3].wait()
    tacc[...] = mm(hid[...].reshape(rows, ch), wtime[2]) + row_of(btime, 0, 2 * ch)

    first = lax.broadcasted_iota(jnp.int32, (width, ch), 0) == 0
    final = lax.broadcasted_iota(jnp.int32, (width, ch), 0) == width - 1

    def spread(index, row):
        for f in range(2):
            value = row[:, f * ch : (f + 1) * ch]
            wider = value.astype(F32)
            abuf[index, f, :, :ch] = jnp.where(first, 0.0, pltpu.roll(wider, 1, 0)).astype(BF16)
            abuf[index, f, :, ch : 2 * ch] = value
            abuf[index, f, :, 2 * ch :] = jnp.where(
                final, 0.0, pltpu.roll(wider, width - 1, 0)
            ).astype(BF16)

    n_space = 2 * chips

    def edge(r, target):
        return pltpu.make_async_remote_copy(
            src_ref=tim.at[r],
            dst_ref=halo.at[1 - r],
            send_sem=hsend.at[r],
            recv_sem=hrecv.at[1 - r],
            device_id=(t, target),
            device_id_type=MESH,
        )

    for r in range(2):
        @pl.when(t >= 2)
        def _(r=r):
            passed(r, 0, t - 2).wait_recv()

        @pl.when(t >= 1)
        def _(r=r):
            passed(r, 1, t - 1).wait_recv()

        row = (
            tacc[pl.ds(r * width, width), :] + mm(hist[1, r], wtime[1]) + mm(hist[0, r], wtime[0])
        ).astype(BF16)
        tim[r] = row
        goes = (s > 0) if r == 0 else (s < n_space - 1)

        @pl.when(goes)
        def _(r=r):
            edge(r, s - 1 if r == 0 else s + 1).start()

        spread(1 + r, row)

    def convolve(j):
        upper, pr = ((0, 0), (1, 1), (1, 0), (2, 1))[j]
        for pc in range(2):
            value = jnp.concatenate([row_of(bspace, 0, c2), jnp.zeros((1, 256 - c2), F32)], axis=1)
            for dr in range(2):
                lhs = abuf[upper + dr, :, :, pc * ch : (pc + 2) * ch].reshape(rows, 2 * ch)
                value = value + mm_t(lhs, wf[pr, pc, :, 2 * dr * ch : 2 * (dr + 1) * ch])
            for half in range(2):
                for f in range(2):
                    wide[half, f, pl.ds(pc, width, stride=2), :] = value[
                        f * width : (f + 1) * width, half * 128 : (half + 1) * 128
                    ]
        for f in range(2):
            outv[j, f, :, :128] = wide[0, f].astype(BF16)
            outv[j, f, :, 128:] = wide[1, f, :, : c2 - 128].astype(BF16)

    def give(j):
        return pltpu.make_async_copy(outv.at[j], out_h.at[:, j], osem.at[j])

    for j in (1, 2):
        convolve(j)
        give(j).start()

    for side in range(2):
        comes = (s > 0) if side == 0 else (s < n_space - 1)

        @pl.when(comes)
        def _(side=side):
            edge(1 - side, s - 1 if side == 0 else s + 1).wait_recv()

        @pl.when(jnp.logical_not(comes))
        def _(side=side):
            halo[side] = jnp.zeros(halo.shape[1:], BF16)

        spread(3 * side, halo[side])
        convolve(3 * side)
        give(3 * side).start()

    for h in range(2):
        @pl.when(has_hi)
        def _(h=h):
            block(z, c, h, 0, s + 2).wait_send()

        @pl.when(has_lo)
        def _(h=h):
            block(z, c, h, 2, s - 2).wait_send()

        block(z, c, h, 1, sib).wait_send()

    @pl.loop(1, chips)
    def _(d):
        for h in range(2):
            for origin, there, onward, target in (
                (z - d, z - d >= 0, has_hi, s + 2),
                (z + d, z + d <= chips - 1, has_lo, s - 2),
            ):
                @pl.when(there)
                def _(origin=origin, onward=onward, target=target, h=h):
                    @pl.when(onward)
                    def _():
                        block(origin, c, h, 0, target).wait_send()

                    block(origin, c, h, 1, sib).wait_send()

    for h in range(2):
        @pl.when(t < steps - 1)
        def _(h=h):
            passed(h, 1, t + 1).wait_send()

        @pl.when(t < steps - 2)
        def _(h=h):
            passed(h, 0, t + 2).wait_send()

    @pl.when(s > 0)
    def _():
        edge(0, s - 1).wait_send()

    @pl.when(s < n_space - 1)
    def _():
        edge(1, s + 1).wait_send()

    for j in range(4):
        give(j).wait()


def handed_on(source, target, sem):
    moves = [
        pltpu.make_async_copy(source.at[f, j], target.at[f, j], sem.at[f, j])
        for f in range(2)
        for j in range(4)
    ]
    for move in moves:
        move.start()
    for move in moves:
        move.wait()


def solution(mesh):
    chips, steps = mesh.shape["space"] // 2, mesh.shape["tm"]

    def body(frames, cache, gain, wqkv, bqkv, wproj, bproj, wtime, btime, wspace, bspace):
        _, _, width, ch = frames.shape
        c2 = wspace.shape[-1]
        wspace = jnp.swapaxes(wspace, 2, 3)
        cache = cache.reshape((2,) + frames.shape[1:])
        rows = 2 * width
        vmem = pl.BlockSpec(memory_space=pltpu.VMEM)
        away = pl.BlockSpec(memory_space=pl.ANY)
        dma = pltpu.SemaphoreType.DMA
        made = pl.pallas_call(
            functools.partial(kernel, chips, steps),
            out_shape=jax.ShapeDtypeStruct((2, 4, 2 * width, c2), BF16),
            in_specs=[vmem, away, vmem, away, vmem, away, vmem, away, vmem, away, vmem],
            out_specs=away,
            scratch_shapes=[
                pltpu.VMEM((chips, 2, rows, ch), BF16),
                pltpu.VMEM(wqkv.shape, BF16),
                pltpu.VMEM(wproj.shape, BF16),
                pltpu.VMEM(wtime.shape, BF16),
                pltpu.VMEM(wspace.shape, BF16),
                pltpu.VMEM((2, 2, 256, 4 * ch), BF16),
                pltpu.VMEM((rows, ch), BF16),
                pltpu.VMEM((rows, 1), F32),
                pltpu.VMEM((rows, 1), F32),
                pltpu.VMEM((rows, ch), F32),
                pltpu.VMEM((2, width, ch), BF16),
                pltpu.VMEM((2, 2, width, ch), BF16),
                pltpu.VMEM((rows, 2 * ch), F32),
                pltpu.VMEM((2, width, 2 * ch), BF16),
                pltpu.VMEM((2, width, 2 * ch), BF16),
                pltpu.VMEM((4, 2, width, 3 * ch), BF16),
                pltpu.VMEM((2, 2, 2 * width, 128), F32),
                pltpu.VMEM((4, 2, 2 * width, c2), BF16),
                dma((4,)),
                dma((chips, 2, 2)),
                dma((chips, 2, 3)),
                dma((2, 2)),
                dma((2, 2)),
                dma((2,)),
                dma((2,)),
                dma((4,)),
                dma((2,)),
            ],
            compiler_params=pltpu.CompilerParams(
                collective_id=0, has_side_effects=True, vmem_limit_bytes=56 * 2**20
            ),
            cost_estimate=pl.CostEstimate(
                flops=2 * 10**9, bytes_accessed=6 * 10**6, transcendentals=300000
            ),
        )(frames, cache, gain, wqkv, bqkv, wproj, bproj, wtime, btime, wspace, bspace)
        return pl.pallas_call(
            handed_on,
            out_shape=jax.ShapeDtypeStruct(made.shape, BF16),
            in_specs=[away],
            out_specs=away,
            scratch_shapes=[dma((2, 4))],
            compiler_params=pltpu.CompilerParams(vmem_limit_bytes=60 * 2**20),
        )(made)

    return jax.shard_map(
        body,
        mesh=mesh,
        in_specs=(P("tm", "space", None, None), P(None, "space", None, None)) + (P(),) * 9,
        out_specs=P("tm", "space", None, None),
        check_vma=False,
    )
```

```python
import functools

import jax
import jax.numpy as jnp
from jax import lax
from jax.experimental import pallas as pl
from jax.experimental.pallas import tpu as pltpu
from jax.sharding import PartitionSpec as P

EPSILON = 1e-06
F32 = jnp.float32
BF16 = jnp.bfloat16
MESH = pl.DeviceIdType.MESH


def mm(left, right):
    return jnp.dot(left, right, preferred_element_type=F32)


def mm_t(left, right):
    return lax.dot_general(left, right, (((1,), (1,)), ((), ())), preferred_element_type=F32)


def row_of(ref, start, size):
    return ref[...].astype(F32).reshape(1, -1)[:, start : start + size]


def kernel(
    chips, steps,
    frames, cache, gain, wqkv_h, bqkv, wproj_h, bproj, wtime_h, btime, wspace_h, bspace,
    out_h,
    xg, wqkv, wproj, wtime, wspace, wf, qp, best, mass, total, hid, hist, tacc, tim, halo, abuf,
    wide, outv,
    wsem, grecv, gsend, trecv, tsend, hrecv, hsend, osem, csem,
):
    ch = frames.shape[-1]
    width = frames.shape[2]
    rows = 2 * width
    c2 = wspace.shape[2]
    t = lax.axis_index("tm")
    s = lax.axis_index("space")
    z, c = s // 2, s % 2
    has_lo, has_hi = z > 0, z < chips - 1
    sib = z * 2 + (1 - c)

    loads = [
        pltpu.make_async_copy(src, dst, wsem.at[i])
        for i, (src, dst) in enumerate(
            ((wqkv_h, wqkv), (wspace_h, wspace), (wproj_h, wproj), (wtime_h, wtime))
        )
    ]
    for load in loads:
        load.start()

    def cached(source, slot):
        return pltpu.make_async_copy(cache.at[source], hist.at[slot], csem.at[slot])

    @pl.when(t == 0)
    def _():
        cached(0, 0).start()
        cached(1, 1).start()

    @pl.when(t == 1)
    def _():
        cached(1, 0).start()

    barrier = pltpu.get_barrier_semaphore()
    cross = jnp.where(c == 0, s - 1, s + 1)
    has_cross = jnp.where(c == 0, has_lo, has_hi)
    peers = [
        (has_lo, t, s - 2),
        (has_hi, t, s + 2),
        (has_cross, t, cross),
        (t >= 1, t - 1, s),
        (t >= 2, t - 2, s),
        (t < steps - 1, t + 1, s),
        (t < steps - 2, t + 2, s),
    ]
    pl.semaphore_signal(barrier, inc=1, device_id=(t, sib), device_id_type=MESH)
    greeted = jnp.int32(1)
    for there, pt, ps in peers:
        greeted = greeted + there.astype(jnp.int32)

        @pl.when(there)
        def _(pt=pt, ps=ps):
            pl.semaphore_signal(barrier, inc=1, device_id=(pt, ps), device_id_type=MESH)

    for r in range(2):
        value = frames[0, r].astype(F32)
        inverse = lax.rsqrt(jnp.mean(value * value, axis=-1, keepdims=True) + EPSILON)
        xg[z, c, pl.ds(r * width, width), :] = (value * inverse * row_of(gain, 0, ch)).astype(BF16)

    pl.semaphore_wait(barrier, greeted)

    def block(origin, core, h, kind, target):
        piece = xg.at[origin, core, pl.ds(h * width, width), :]
        return pltpu.make_async_remote_copy(
            src_ref=piece,
            dst_ref=piece,
            send_sem=gsend.at[origin, h, kind],
            recv_sem=grecv.at[origin, core, h],
            device_id=(t, target),
            device_id_type=MESH,
        )

    for h in range(2):
        @pl.when(has_hi)
        def _(h=h):
            block(z, c, h, 0, s + 2).start()

        @pl.when(has_lo)
        def _(h=h):
            block(z, c, h, 2, s - 2).start()

        block(z, c, h, 1, sib).start()

    loads[0].wait()
    mine = xg[z, c]
    queries = (mm(mine, wqkv[:, :ch]) + row_of(bqkv, 0, ch)).astype(BF16)
    scale = ch ** (-0.5)
    qp[...] = (mm_t(queries, wqkv[:, ch : 2 * ch]) * scale).astype(BF16)
    offset = jnp.sum(queries.astype(F32) * row_of(bqkv, ch, ch), axis=1, keepdims=True) * scale

    def scores_of(origin):
        keys = xg[origin].reshape(2 * rows, ch)
        return keys, mm_t(qp[...], keys) + offset

    for h in range(2):
        block(z, 1 - c, h, 1, sib).wait_recv()
    keys, scores = scores_of(z)
    top = jnp.max(scores, axis=1, keepdims=True)
    weights = jnp.exp(scores - top)
    best[...] = top
    mass[...] = jnp.sum(weights, axis=1, keepdims=True)
    total[...] = mm(weights.astype(BF16), keys)

    def absorb(origin):
        keys, scores = scores_of(origin)
        top = jnp.maximum(best[...], jnp.max(scores, axis=1, keepdims=True))
        weights = jnp.exp(scores - top)
        shrink = jnp.exp(best[...] - top)
        best[...] = top
        mass[...] = mass[...] * shrink + jnp.sum(weights, axis=1, keepdims=True)
        total[...] = total[...] * shrink + mm(weights.astype(BF16), keys)

    def sides_of(d):
        return (
            (z - d, z - d >= 0, has_hi, s + 2),
            (z + d, z + d <= chips - 1, has_lo, s - 2),
        )

    def forward(d):
        for h in range(2):
            for origin, there, onward, target in sides_of(d):
                @pl.when(there)
                def _(origin=origin, onward=onward, target=target, h=h):
                    block(origin, c, h, 1, sib).wait_recv()

                    @pl.when(onward)
                    def _():
                        block(origin, c, h, 0, target).start()

                    block(origin, c, h, 1, sib).start()

    def take(d):
        for origin, there, onward, target in sides_of(d):
            @pl.when(there)
            def _(origin=origin):
                for h in range(2):
                    block(origin, 1 - c, h, 1, sib).wait_recv()
                absorb(origin)

    forward(1)

    loads[1].wait()
    groups = (((0,), (1, 2)), ((0, 1), (2,)))
    for pr in range(2):
        for pc in range(2):
            for dr in range(2):
                for dc in range(2):
                    part = None
                    for i in groups[pr][dr]:
                        for j in groups[pc][dc]:
                            tap = wspace[i, j].astype(F32)
                            part = tap if part is None else part + tap
                    at = (2 * dr + dc) * ch
                    wf[pr, pc, :c2, at : at + ch] = part.astype(BF16)
            wf[pr, pc, c2:, :] = jnp.zeros((256 - c2, 4 * ch), BF16)

    take(1)

    @pl.loop(2, chips)
    def _(d):
        forward(d)
        take(d)

    loads[2].wait()

    def passed(h, kind, target):
        return pltpu.make_async_remote_copy(
            src_ref=hid.at[h],
            dst_ref=hist.at[kind, h],
            send_sem=tsend.at[kind, h],
            recv_sem=trecv.at[kind, h],
            device_id=(target, s),
            device_id_type=MESH,
        )

    for h in range(2):
        at = pl.ds(h * width, width)
        rows_mixed = (total[at, :] / mass[at, :]).astype(BF16)
        mixed = (mm(rows_mixed, wqkv[:, 2 * ch :]) + row_of(bqkv, 2 * ch, ch)).astype(BF16)
        hid[h] = (
            frames[0, h].astype(F32) + mm(mixed, wproj[...]) + row_of(bproj, 0, ch)
        ).astype(BF16)

        @pl.when(t < steps - 1)
        def _(h=h):
            passed(h, 1, t + 1).start()

        @pl.when(t < steps - 2)
        def _(h=h):
            passed(h, 0, t + 2).start()

    @pl.when(t == 0)
    def _():
        cached(0, 0).wait()
        cached(1, 1).wait()

    @pl.when(t == 1)
    def _():
        cached(1, 0).wait()

    loads[3].wait()
    tacc[...] = mm(hid[...].reshape(rows, ch), wtime[2]) + row_of(btime, 0, 2 * ch)

    first = lax.broadcasted_iota(jnp.int32, (width, ch), 0) == 0
    final = lax.broadcasted_iota(jnp.int32, (width, ch), 0) == width - 1

    def spread(index, row):
        for f in range(2):
            value = row[:, f * ch : (f + 1) * ch]
            wider = value.astype(F32)
            abuf[index, f, :, :ch] = jnp.where(first, 0.0, pltpu.roll(wider, 1, 0)).astype(BF16)
            abuf[index, f, :, ch : 2 * ch] = value
            abuf[index, f, :, 2 * ch :] = jnp.where(
                final, 0.0, pltpu.roll(wider, width - 1, 0)
            ).astype(BF16)

    n_space = 2 * chips

    def edge(r, target):
        return pltpu.make_async_remote_copy(
            src_ref=tim.at[r],
            dst_ref=halo.at[1 - r],
            send_sem=hsend.at[r],
            recv_sem=hrecv.at[1 - r],
            device_id=(t, target),
            device_id_type=MESH,
        )

    for r in range(2):
        @pl.when(t >= 2)
        def _(r=r):
            passed(r, 0, t - 2).wait_recv()

        @pl.when(t >= 1)
        def _(r=r):
            passed(r, 1, t - 1).wait_recv()

        row = (
            tacc[pl.ds(r * width, width), :] + mm(hist[1, r], wtime[1]) + mm(hist[0, r], wtime[0])
        ).astype(BF16)
        tim[r] = row
        goes = (s > 0) if r == 0 else (s < n_space - 1)

        @pl.when(goes)
        def _(r=r):
            edge(r, s - 1 if r == 0 else s + 1).start()

        spread(1 + r, row)

    def convolve(j):
        upper, pr = ((0, 0), (1, 1), (1, 0), (2, 1))[j]
        for pc in range(2):
            value = jnp.concatenate([row_of(bspace, 0, c2), jnp.zeros((1, 256 - c2), F32)], axis=1)
            for dr in range(2):
                lhs = abuf[upper + dr, :, :, pc * ch : (pc + 2) * ch].reshape(rows, 2 * ch)
                value = value + mm_t(lhs, wf[pr, pc, :, 2 * dr * ch : 2 * (dr + 1) * ch])
            for half in range(2):
                for f in range(2):
                    wide[half, f, pl.ds(pc, width, stride=2), :] = value[
                        f * width : (f + 1) * width, half * 128 : (half + 1) * 128
                    ]
        for f in range(2):
            outv[j, f, :, :128] = wide[0, f].astype(BF16)
            outv[j, f, :, 128:] = wide[1, f, :, : c2 - 128].astype(BF16)

    def give(j):
        return pltpu.make_async_copy(outv.at[j], out_h.at[:, j], osem.at[j])

    for j in (1, 2):
        convolve(j)
        give(j).start()

    for side in range(2):
        comes = (s > 0) if side == 0 else (s < n_space - 1)

        @pl.when(comes)
        def _(side=side):
            edge(1 - side, s - 1 if side == 0 else s + 1).wait_recv()

        @pl.when(jnp.logical_not(comes))
        def _(side=side):
            halo[side] = jnp.zeros(halo.shape[1:], BF16)

        spread(3 * side, halo[side])
        convolve(3 * side)
        give(3 * side).start()

    for h in range(2):
        @pl.when(has_hi)
        def _(h=h):
            block(z, c, h, 0, s + 2).wait_send()

        @pl.when(has_lo)
        def _(h=h):
            block(z, c, h, 2, s - 2).wait_send()

        block(z, c, h, 1, sib).wait_send()

    @pl.loop(1, chips)
    def _(d):
        for h in range(2):
            for origin, there, onward, target in (
                (z - d, z - d >= 0, has_hi, s + 2),
                (z + d, z + d <= chips - 1, has_lo, s - 2),
            ):
                @pl.when(there)
                def _(origin=origin, onward=onward, target=target, h=h):
                    @pl.when(onward)
                    def _():
                        block(origin, c, h, 0, target).wait_send()

                    block(origin, c, h, 1, sib).wait_send()

    for h in range(2):
        @pl.when(t < steps - 1)
        def _(h=h):
            passed(h, 1, t + 1).wait_send()

        @pl.when(t < steps - 2)
        def _(h=h):
            passed(h, 0, t + 2).wait_send()

    @pl.when(s > 0)
    def _():
        edge(0, s - 1).wait_send()

    @pl.when(s < n_space - 1)
    def _():
        edge(1, s + 1).wait_send()

    for j in range(4):
        give(j).wait()


def handed_on(source, target, held, into, out):
    places = [(f, j) for f in range(2) for j in range(4)]
    comes = [
        pltpu.make_async_copy(source.at[f, j], held.at[f, j], into.at[f, j]) for f, j in places
    ]
    goes = [pltpu.make_async_copy(held.at[f, j], target.at[f, j], out.at[f, j]) for f, j in places]
    for come in comes:
        come.start()
    for come, go in zip(comes, goes):
        come.wait()
        go.start()
    for go in goes:
        go.wait()


def solution(mesh):
    chips, steps = mesh.shape["space"] // 2, mesh.shape["tm"]

    def body(frames, cache, gain, wqkv, bqkv, wproj, bproj, wtime, btime, wspace, bspace):
        _, _, width, ch = frames.shape
        c2 = wspace.shape[-1]
        wspace = jnp.swapaxes(wspace, 2, 3)
        cache = cache.reshape((2,) + frames.shape[1:])
        rows = 2 * width
        vmem = pl.BlockSpec(memory_space=pltpu.VMEM)
        away = pl.BlockSpec(memory_space=pl.ANY)
        dma = pltpu.SemaphoreType.DMA
        made = pl.pallas_call(
            functools.partial(kernel, chips, steps),
            out_shape=jax.ShapeDtypeStruct((2, 4, 2 * width, c2), BF16),
            in_specs=[vmem, away, vmem, away, vmem, away, vmem, away, vmem, away, vmem],
            out_specs=away,
            scratch_shapes=[
                pltpu.VMEM((chips, 2, rows, ch), BF16),
                pltpu.VMEM(wqkv.shape, BF16),
                pltpu.VMEM(wproj.shape, BF16),
                pltpu.VMEM(wtime.shape, BF16),
                pltpu.VMEM(wspace.shape, BF16),
                pltpu.VMEM((2, 2, 256, 4 * ch), BF16),
                pltpu.VMEM((rows, ch), BF16),
                pltpu.VMEM((rows, 1), F32),
                pltpu.VMEM((rows, 1), F32),
                pltpu.VMEM((rows, ch), F32),
                pltpu.VMEM((2, width, ch), BF16),
                pltpu.VMEM((2, 2, width, ch), BF16),
                pltpu.VMEM((rows, 2 * ch), F32),
                pltpu.VMEM((2, width, 2 * ch), BF16),
                pltpu.VMEM((2, width, 2 * ch), BF16),
                pltpu.VMEM((4, 2, width, 3 * ch), BF16),
                pltpu.VMEM((2, 2, 2 * width, 128), F32),
                pltpu.VMEM((4, 2, 2 * width, c2), BF16),
                dma((4,)),
                dma((chips, 2, 2)),
                dma((chips, 2, 3)),
                dma((2, 2)),
                dma((2, 2)),
                dma((2,)),
                dma((2,)),
                dma((4,)),
                dma((2,)),
            ],
            compiler_params=pltpu.CompilerParams(
                collective_id=0, has_side_effects=True, vmem_limit_bytes=56 * 2**20
            ),
            cost_estimate=pl.CostEstimate(
                flops=2 * 10**9, bytes_accessed=6 * 10**6, transcendentals=300000
            ),
        )(frames, cache, gain, wqkv, bqkv, wproj, bproj, wtime, btime, wspace, bspace)
        return pl.pallas_call(
            handed_on,
            out_shape=jax.ShapeDtypeStruct(made.shape, BF16),
            in_specs=[away],
            out_specs=away,
            scratch_shapes=[pltpu.VMEM(made.shape, BF16), dma((2, 4)), dma((2, 4))],
            compiler_params=pltpu.CompilerParams(vmem_limit_bytes=60 * 2**20),
        )(made)

    return jax.shard_map(
        body,
        mesh=mesh,
        in_specs=(P("tm", "space", None, None), P(None, "space", None, None)) + (P(),) * 9,
        out_specs=P("tm", "space", None, None),
        check_vma=False,
    )
```

```python
import functools

import jax
import jax.numpy as jnp
from jax import lax
from jax.experimental import pallas as pl
from jax.experimental.pallas import tpu as pltpu
from jax.sharding import PartitionSpec as P

EPSILON = 1e-06
F32 = jnp.float32
BF16 = jnp.bfloat16
MESH = pl.DeviceIdType.MESH


def mm(left, right):
    return jnp.dot(left, right, preferred_element_type=F32)


def mm_t(left, right):
    return lax.dot_general(left, right, (((1,), (1,)), ((), ())), preferred_element_type=F32)


def row_of(ref, start, size):
    return ref[...].astype(F32).reshape(1, -1)[:, start : start + size]


def kernel(
    chips, steps,
    frames, cache, gain, wqkv_h, bqkv, wproj_h, bproj, wtime_h, btime, wspace_h, bspace,
    out_h,
    xg, wqkv, wproj, wtime, wspace, wf, qp, best, mass, total, hid, hist, tacc, tim, halo, abuf,
    wide, outv,
    wsem, grecv, gsend, trecv, tsend, hrecv, hsend, osem, csem,
):
    ch = frames.shape[-1]
    width = frames.shape[2]
    rows = 2 * width
    c2 = wspace.shape[2]
    t = lax.axis_index("tm")
    s = lax.axis_index("space")
    z, c = s // 2, s % 2
    has_lo, has_hi = z > 0, z < chips - 1
    sib = z * 2 + (1 - c)

    loads = [
        pltpu.make_async_copy(src, dst, wsem.at[i])
        for i, (src, dst) in enumerate(
            ((wqkv_h, wqkv), (wspace_h, wspace), (wproj_h, wproj), (wtime_h, wtime))
        )
    ]
    for load in loads:
        load.start()

    def cached(source, slot):
        return pltpu.make_async_copy(cache.at[source], hist.at[slot], csem.at[slot])

    @pl.when(t == 0)
    def _():
        cached(0, 0).start()
        cached(1, 1).start()

    @pl.when(t == 1)
    def _():
        cached(1, 0).start()

    barrier = pltpu.get_barrier_semaphore()
    cross = jnp.where(c == 0, s - 1, s + 1)
    has_cross = jnp.where(c == 0, has_lo, has_hi)
    peers = [
        (has_lo, t, s - 2),
        (has_hi, t, s + 2),
        (has_cross, t, cross),
        (t >= 1, t - 1, s),
        (t >= 2, t - 2, s),
        (t < steps - 1, t + 1, s),
        (t < steps - 2, t + 2, s),
    ]
    pl.semaphore_signal(barrier, inc=1, device_id=(t, sib), device_id_type=MESH)
    greeted = jnp.int32(1)
    for there, pt, ps in peers:
        greeted = greeted + there.astype(jnp.int32)

        @pl.when(there)
        def _(pt=pt, ps=ps):
            pl.semaphore_signal(barrier, inc=1, device_id=(pt, ps), device_id_type=MESH)

    for r in range(2):
        value = frames[0, r].astype(F32)
        inverse = lax.rsqrt(jnp.mean(value * value, axis=-1, keepdims=True) + EPSILON)
        xg[z, c, pl.ds(r * width, width), :] = (value * inverse * row_of(gain, 0, ch)).astype(BF16)

    pl.semaphore_wait(barrier, greeted)

    def block(origin, core, h, kind, target):
        piece = xg.at[origin, core, pl.ds(h * width, width), :]
        return pltpu.make_async_remote_copy(
            src_ref=piece,
            dst_ref=piece,
            send_sem=gsend.at[origin, h, kind],
            recv_sem=grecv.at[origin, core, h],
            device_id=(t, target),
            device_id_type=MESH,
        )

    for h in range(2):
        @pl.when(has_hi)
        def _(h=h):
            block(z, c, h, 0, s + 2).start()

        @pl.when(has_lo)
        def _(h=h):
            block(z, c, h, 2, s - 2).start()

        block(z, c, h, 1, sib).start()

    loads[0].wait()
    mine = xg[z, c]
    queries = (mm(mine, wqkv[:, :ch]) + row_of(bqkv, 0, ch)).astype(BF16)
    scale = ch ** (-0.5)
    qp[...] = (mm_t(queries, wqkv[:, ch : 2 * ch]) * scale).astype(BF16)
    offset = jnp.sum(queries.astype(F32) * row_of(bqkv, ch, ch), axis=1, keepdims=True) * scale

    def scores_of(origin):
        keys = xg[origin].reshape(2 * rows, ch)
        return keys, mm_t(qp[...], keys) + offset

    for h in range(2):
        block(z, 1 - c, h, 1, sib).wait_recv()
    keys, scores = scores_of(z)
    top = jnp.max(scores, axis=1, keepdims=True)
    weights = jnp.exp(scores - top)
    best[...] = top
    mass[...] = jnp.sum(weights, axis=1, keepdims=True)
    total[...] = mm(weights.astype(BF16), keys)

    def absorb(origin):
        keys, scores = scores_of(origin)
        top = jnp.maximum(best[...], jnp.max(scores, axis=1, keepdims=True))
        weights = jnp.exp(scores - top)
        shrink = jnp.exp(best[...] - top)
        best[...] = top
        mass[...] = mass[...] * shrink + jnp.sum(weights, axis=1, keepdims=True)
        total[...] = total[...] * shrink + mm(weights.astype(BF16), keys)

    def sides_of(d):
        return (
            (z - d, z - d >= 0, has_hi, s + 2),
            (z + d, z + d <= chips - 1, has_lo, s - 2),
        )

    def forward(d):
        for h in range(2):
            for origin, there, onward, target in sides_of(d):
                @pl.when(there)
                def _(origin=origin, onward=onward, target=target, h=h):
                    block(origin, c, h, 1, sib).wait_recv()

                    @pl.when(onward)
                    def _():
                        block(origin, c, h, 0, target).start()

                    block(origin, c, h, 1, sib).start()

    def take(d):
        for origin, there, onward, target in sides_of(d):
            @pl.when(there)
            def _(origin=origin):
                for h in range(2):
                    block(origin, 1 - c, h, 1, sib).wait_recv()
                absorb(origin)

    forward(1)

    loads[1].wait()
    groups = (((0,), (1, 2)), ((0, 1), (2,)))
    def fold(pr):
        for pc in range(2):
            for dr in range(2):
                for dc in range(2):
                    part = None
                    for i in groups[pr][dr]:
                        for j in groups[pc][dc]:
                            tap = wspace[i, j].astype(F32)
                            part = tap if part is None else part + tap
                    at = (2 * dr + dc) * ch
                    wf[pr, pc, :c2, at : at + ch] = part.astype(BF16)
            wf[pr, pc, c2:, :] = jnp.zeros((256 - c2, 4 * ch), BF16)

    fold(0)
    take(1)
    forward(2)
    fold(1)
    take(2)

    @pl.loop(3, chips)
    def _(d):
        forward(d)
        take(d)

    loads[2].wait()

    def passed(h, kind, target):
        return pltpu.make_async_remote_copy(
            src_ref=hid.at[h],
            dst_ref=hist.at[kind, h],
            send_sem=tsend.at[kind, h],
            recv_sem=trecv.at[kind, h],
            device_id=(target, s),
            device_id_type=MESH,
        )

    for h in range(2):
        at = pl.ds(h * width, width)
        rows_mixed = (total[at, :] / mass[at, :]).astype(BF16)
        mixed = (mm(rows_mixed, wqkv[:, 2 * ch :]) + row_of(bqkv, 2 * ch, ch)).astype(BF16)
        hid[h] = (
            frames[0, h].astype(F32) + mm(mixed, wproj[...]) + row_of(bproj, 0, ch)
        ).astype(BF16)

        @pl.when(t < steps - 1)
        def _(h=h):
            passed(h, 1, t + 1).start()

        @pl.when(t < steps - 2)
        def _(h=h):
            passed(h, 0, t + 2).start()

    @pl.when(t == 0)
    def _():
        cached(0, 0).wait()
        cached(1, 1).wait()

    @pl.when(t == 1)
    def _():
        cached(1, 0).wait()

    loads[3].wait()
    tacc[...] = mm(hid[...].reshape(rows, ch), wtime[2]) + row_of(btime, 0, 2 * ch)

    first = lax.broadcasted_iota(jnp.int32, (width, ch), 0) == 0
    final = lax.broadcasted_iota(jnp.int32, (width, ch), 0) == width - 1

    def spread(index, row):
        for f in range(2):
            value = row[:, f * ch : (f + 1) * ch]
            wider = value.astype(F32)
            abuf[index, f, :, :ch] = jnp.where(first, 0.0, pltpu.roll(wider, 1, 0)).astype(BF16)
            abuf[index, f, :, ch : 2 * ch] = value
            abuf[index, f, :, 2 * ch :] = jnp.where(
                final, 0.0, pltpu.roll(wider, width - 1, 0)
            ).astype(BF16)

    n_space = 2 * chips

    def edge(r, target):
        return pltpu.make_async_remote_copy(
            src_ref=tim.at[r],
            dst_ref=halo.at[1 - r],
            send_sem=hsend.at[r],
            recv_sem=hrecv.at[1 - r],
            device_id=(t, target),
            device_id_type=MESH,
        )

    for r in range(2):
        @pl.when(t >= 2)
        def _(r=r):
            passed(r, 0, t - 2).wait_recv()

        @pl.when(t >= 1)
        def _(r=r):
            passed(r, 1, t - 1).wait_recv()

        row = (
            tacc[pl.ds(r * width, width), :] + mm(hist[1, r], wtime[1]) + mm(hist[0, r], wtime[0])
        ).astype(BF16)
        tim[r] = row
        goes = (s > 0) if r == 0 else (s < n_space - 1)

        @pl.when(goes)
        def _(r=r):
            edge(r, s - 1 if r == 0 else s + 1).start()

        spread(1 + r, row)

    def convolve(j):
        upper, pr = ((0, 0), (1, 1), (1, 0), (2, 1))[j]
        for pc in range(2):
            value = jnp.concatenate([row_of(bspace, 0, c2), jnp.zeros((1, 256 - c2), F32)], axis=1)
            for dr in range(2):
                lhs = abuf[upper + dr, :, :, pc * ch : (pc + 2) * ch].reshape(rows, 2 * ch)
                value = value + mm_t(lhs, wf[pr, pc, :, 2 * dr * ch : 2 * (dr + 1) * ch])
            for half in range(2):
                for f in range(2):
                    wide[half, f, pl.ds(pc, width, stride=2), :] = value[
                        f * width : (f + 1) * width, half * 128 : (half + 1) * 128
                    ]
        for f in range(2):
            outv[j, f, :, :128] = wide[0, f].astype(BF16)
            outv[j, f, :, 128:] = wide[1, f, :, : c2 - 128].astype(BF16)

    def give(j):
        return pltpu.make_async_copy(outv.at[j], out_h.at[:, j], osem.at[j])

    for j in (1, 2):
        convolve(j)
        give(j).start()

    for side in range(2):
        comes = (s > 0) if side == 0 else (s < n_space - 1)

        @pl.when(comes)
        def _(side=side):
            edge(1 - side, s - 1 if side == 0 else s + 1).wait_recv()

        @pl.when(jnp.logical_not(comes))
        def _(side=side):
            halo[side] = jnp.zeros(halo.shape[1:], BF16)

        spread(3 * side, halo[side])
        convolve(3 * side)
        give(3 * side).start()

    for h in range(2):
        @pl.when(has_hi)
        def _(h=h):
            block(z, c, h, 0, s + 2).wait_send()

        @pl.when(has_lo)
        def _(h=h):
            block(z, c, h, 2, s - 2).wait_send()

        block(z, c, h, 1, sib).wait_send()

    @pl.loop(1, chips)
    def _(d):
        for h in range(2):
            for origin, there, onward, target in (
                (z - d, z - d >= 0, has_hi, s + 2),
                (z + d, z + d <= chips - 1, has_lo, s - 2),
            ):
                @pl.when(there)
                def _(origin=origin, onward=onward, target=target, h=h):
                    @pl.when(onward)
                    def _():
                        block(origin, c, h, 0, target).wait_send()

                    block(origin, c, h, 1, sib).wait_send()

    for h in range(2):
        @pl.when(t < steps - 1)
        def _(h=h):
            passed(h, 1, t + 1).wait_send()

        @pl.when(t < steps - 2)
        def _(h=h):
            passed(h, 0, t + 2).wait_send()

    @pl.when(s > 0)
    def _():
        edge(0, s - 1).wait_send()

    @pl.when(s < n_space - 1)
    def _():
        edge(1, s + 1).wait_send()

    for j in range(4):
        give(j).wait()


def handed_on(source, target, held, into, out):
    places = [(f, j) for f in range(2) for j in range(4)]
    comes = [
        pltpu.make_async_copy(source.at[f, j], held.at[f, j], into.at[f, j]) for f, j in places
    ]
    goes = [pltpu.make_async_copy(held.at[f, j], target.at[f, j], out.at[f, j]) for f, j in places]
    for come in comes:
        come.start()
    for come, go in zip(comes, goes):
        come.wait()
        go.start()
    for go in goes:
        go.wait()


def solution(mesh):
    chips, steps = mesh.shape["space"] // 2, mesh.shape["tm"]

    def body(frames, cache, gain, wqkv, bqkv, wproj, bproj, wtime, btime, wspace, bspace):
        _, _, width, ch = frames.shape
        c2 = wspace.shape[-1]
        wspace = jnp.swapaxes(wspace, 2, 3)
        cache = cache.reshape((2,) + frames.shape[1:])
        rows = 2 * width
        vmem = pl.BlockSpec(memory_space=pltpu.VMEM)
        away = pl.BlockSpec(memory_space=pl.ANY)
        dma = pltpu.SemaphoreType.DMA
        made = pl.pallas_call(
            functools.partial(kernel, chips, steps),
            out_shape=jax.ShapeDtypeStruct((2, 4, 2 * width, c2), BF16),
            in_specs=[vmem, away, vmem, away, vmem, away, vmem, away, vmem, away, vmem],
            out_specs=away,
            scratch_shapes=[
                pltpu.VMEM((chips, 2, rows, ch), BF16),
                pltpu.VMEM(wqkv.shape, BF16),
                pltpu.VMEM(wproj.shape, BF16),
                pltpu.VMEM(wtime.shape, BF16),
                pltpu.VMEM(wspace.shape, BF16),
                pltpu.VMEM((2, 2, 256, 4 * ch), BF16),
                pltpu.VMEM((rows, ch), BF16),
                pltpu.VMEM((rows, 1), F32),
                pltpu.VMEM((rows, 1), F32),
                pltpu.VMEM((rows, ch), F32),
                pltpu.VMEM((2, width, ch), BF16),
                pltpu.VMEM((2, 2, width, ch), BF16),
                pltpu.VMEM((rows, 2 * ch), F32),
                pltpu.VMEM((2, width, 2 * ch), BF16),
                pltpu.VMEM((2, width, 2 * ch), BF16),
                pltpu.VMEM((4, 2, width, 3 * ch), BF16),
                pltpu.VMEM((2, 2, 2 * width, 128), F32),
                pltpu.VMEM((4, 2, 2 * width, c2), BF16),
                dma((4,)),
                dma((chips, 2, 2)),
                dma((chips, 2, 3)),
                dma((2, 2)),
                dma((2, 2)),
                dma((2,)),
                dma((2,)),
                dma((4,)),
                dma((2,)),
            ],
            compiler_params=pltpu.CompilerParams(
                collective_id=0, has_side_effects=True, vmem_limit_bytes=56 * 2**20
            ),
            cost_estimate=pl.CostEstimate(
                flops=2 * 10**9, bytes_accessed=6 * 10**6, transcendentals=300000
            ),
        )(frames, cache, gain, wqkv, bqkv, wproj, bproj, wtime, btime, wspace, bspace)
        return pl.pallas_call(
            handed_on,
            out_shape=jax.ShapeDtypeStruct(made.shape, BF16),
            in_specs=[away],
            out_specs=away,
            scratch_shapes=[pltpu.VMEM(made.shape, BF16), dma((2, 4)), dma((2, 4))],
            compiler_params=pltpu.CompilerParams(vmem_limit_bytes=60 * 2**20),
        )(made)

    return jax.shard_map(
        body,
        mesh=mesh,
        in_specs=(P("tm", "space", None, None), P(None, "space", None, None)) + (P(),) * 9,
        out_specs=P("tm", "space", None, None),
        check_vma=False,
    )
```

```python
import functools

import jax
import jax.numpy as jnp
from jax import lax
from jax.experimental import pallas as pl
from jax.experimental.pallas import tpu as pltpu
from jax.sharding import PartitionSpec as P

EPSILON = 1e-06
F32 = jnp.float32
BF16 = jnp.bfloat16
MESH = pl.DeviceIdType.MESH


def mm(left, right):
    return jnp.dot(left, right, preferred_element_type=F32)


def mm_t(left, right):
    return lax.dot_general(left, right, (((1,), (1,)), ((), ())), preferred_element_type=F32)


def row_of(ref, start, size):
    return ref[...].astype(F32).reshape(1, -1)[:, start : start + size]


def kernel(
    chips, steps,
    frames, cache, gain, wqkv_h, bqkv, wproj_h, bproj, wtime_h, btime, wspace_h, bspace,
    out_h,
    xg, wqkv, wproj, wtime, wspace, wf, qp, best, mass, total, hid, hist, tacc, tim, halo, abuf,
    wide, outv,
    wsem, grecv, gsend, trecv, tsend, hrecv, hsend, osem, csem,
):
    ch = frames.shape[-1]
    width = frames.shape[2]
    rows = 2 * width
    c2 = wspace.shape[2]
    t = lax.axis_index("tm")
    s = lax.axis_index("space")
    z, c = s // 2, s % 2
    has_lo, has_hi = z > 0, z < chips - 1
    sib = z * 2 + (1 - c)

    loads = [
        pltpu.make_async_copy(src, dst, wsem.at[i])
        for i, (src, dst) in enumerate(
            ((wqkv_h, wqkv), (wspace_h, wspace), (wproj_h, wproj), (wtime_h, wtime))
        )
    ]
    for load in loads:
        load.start()

    def cached(source, slot):
        return pltpu.make_async_copy(cache.at[source], hist.at[slot], csem.at[slot])

    @pl.when(t == 0)
    def _():
        cached(0, 0).start()
        cached(1, 1).start()

    @pl.when(t == 1)
    def _():
        cached(1, 0).start()

    barrier = pltpu.get_barrier_semaphore()
    cross = jnp.where(c == 0, s - 1, s + 1)
    has_cross = jnp.where(c == 0, has_lo, has_hi)
    peers = [
        (has_lo, t, s - 2),
        (has_hi, t, s + 2),
        (has_cross, t, cross),
        (t >= 1, t - 1, s),
        (t >= 2, t - 2, s),
        (t < steps - 1, t + 1, s),
        (t < steps - 2, t + 2, s),
    ]
    pl.semaphore_signal(barrier, inc=1, device_id=(t, sib), device_id_type=MESH)
    greeted = jnp.int32(1)
    for there, pt, ps in peers:
        greeted = greeted + there.astype(jnp.int32)

        @pl.when(there)
        def _(pt=pt, ps=ps):
            pl.semaphore_signal(barrier, inc=1, device_id=(pt, ps), device_id_type=MESH)

    for r in range(2):
        value = frames[0, r].astype(F32)
        inverse = lax.rsqrt(jnp.mean(value * value, axis=-1, keepdims=True) + EPSILON)
        xg[z, c, pl.ds(r * width, width), :] = (value * inverse * row_of(gain, 0, ch)).astype(BF16)

    pl.semaphore_wait(barrier, greeted)

    def block(origin, core, h, kind, target):
        piece = xg.at[origin, core, pl.ds(h * width, width), :]
        return pltpu.make_async_remote_copy(
            src_ref=piece,
            dst_ref=piece,
            send_sem=gsend.at[origin, h, kind],
            recv_sem=grecv.at[origin, core, h],
            device_id=(t, target),
            device_id_type=MESH,
        )

    for h in range(2):
        @pl.when(has_hi)
        def _(h=h):
            block(z, c, h, 0, s + 2).start()

        @pl.when(has_lo)
        def _(h=h):
            block(z, c, h, 2, s - 2).start()

        block(z, c, h, 1, sib).start()

    loads[0].wait()
    mine = xg[z, c]
    queries = (mm(mine, wqkv[:, :ch]) + row_of(bqkv, 0, ch)).astype(BF16)
    scale = ch ** (-0.5)
    qp[...] = (mm_t(queries, wqkv[:, ch : 2 * ch]) * scale).astype(BF16)
    offset = jnp.sum(queries.astype(F32) * row_of(bqkv, ch, ch), axis=1, keepdims=True) * scale

    def scores_of(origin):
        keys = xg[origin].reshape(2 * rows, ch)
        return keys, mm_t(qp[...], keys) + offset

    for h in range(2):
        block(z, 1 - c, h, 1, sib).wait_recv()
    keys, scores = scores_of(z)
    top = jnp.max(scores, axis=1, keepdims=True)
    weights = jnp.exp(scores - top)
    best[...] = top
    mass[...] = jnp.sum(weights, axis=1, keepdims=True)
    total[...] = mm(weights.astype(BF16), keys)

    def absorb(origin):
        keys, scores = scores_of(origin)
        top = jnp.maximum(best[...], jnp.max(scores, axis=1, keepdims=True))
        weights = jnp.exp(scores - top)
        shrink = jnp.exp(best[...] - top)
        best[...] = top
        mass[...] = mass[...] * shrink + jnp.sum(weights, axis=1, keepdims=True)
        total[...] = total[...] * shrink + mm(weights.astype(BF16), keys)

    def sides_of(d):
        return (
            (z - d, z - d >= 0, has_hi, s + 2),
            (z + d, z + d <= chips - 1, has_lo, s - 2),
        )

    def forward(d):
        for h in range(2):
            for origin, there, onward, target in sides_of(d):
                @pl.when(there)
                def _(origin=origin, onward=onward, target=target, h=h):
                    block(origin, c, h, 1, sib).wait_recv()

                    @pl.when(onward)
                    def _():
                        block(origin, c, h, 0, target).start()

                    block(origin, c, h, 1, sib).start()

    def take(d):
        for origin, there, onward, target in sides_of(d):
            @pl.when(there)
            def _(origin=origin):
                for h in range(2):
                    block(origin, 1 - c, h, 1, sib).wait_recv()
                absorb(origin)

    forward(1)

    loads[1].wait()
    groups = (((0,), (1, 2)), ((0, 1), (2,)))
    for pr in range(2):
        for pc in range(2):
            for dr in range(2):
                for dc in range(2):
                    part = None
                    for i in groups[pr][dr]:
                        for j in groups[pc][dc]:
                            tap = wspace[i, j].astype(F32)
                            part = tap if part is None else part + tap
                    at = (2 * dr + dc) * ch
                    wf[pr, pc, :c2, at : at + ch] = part.astype(BF16)
            wf[pr, pc, c2:, :] = jnp.zeros((256 - c2, 4 * ch), BF16)

    take(1)

    @pl.loop(2, chips)
    def _(d):
        forward(d)
        take(d)

    loads[2].wait()

    def passed(h, kind, target):
        return pltpu.make_async_remote_copy(
            src_ref=hid.at[h],
            dst_ref=hist.at[kind, h],
            send_sem=tsend.at[kind, h],
            recv_sem=trecv.at[kind, h],
            device_id=(target, s),
            device_id_type=MESH,
        )

    for h in range(2):
        at = pl.ds(h * width, width)
        rows_mixed = (total[at, :] / mass[at, :]).astype(BF16)
        mixed = (mm(rows_mixed, wqkv[:, 2 * ch :]) + row_of(bqkv, 2 * ch, ch)).astype(BF16)
        hid[h] = (
            frames[0, h].astype(F32) + mm(mixed, wproj[...]) + row_of(bproj, 0, ch)
        ).astype(BF16)

        @pl.when(t < steps - 1)
        def _(h=h):
            passed(h, 1, t + 1).start()

        @pl.when(t < steps - 2)
        def _(h=h):
            passed(h, 0, t + 2).start()

    @pl.when(t == 0)
    def _():
        cached(0, 0).wait()
        cached(1, 1).wait()

    @pl.when(t == 1)
    def _():
        cached(1, 0).wait()

    loads[3].wait()
    tacc[...] = mm(hid[...].reshape(rows, ch), wtime[2]) + row_of(btime, 0, 2 * ch)

    first = lax.broadcasted_iota(jnp.int32, (width, ch), 0) == 0
    final = lax.broadcasted_iota(jnp.int32, (width, ch), 0) == width - 1

    def spread(index, row):
        for f in range(2):
            value = row[:, f * ch : (f + 1) * ch]
            wider = value.astype(F32)
            abuf[index, f, :, :ch] = jnp.where(first, 0.0, pltpu.roll(wider, 1, 0)).astype(BF16)
            abuf[index, f, :, ch : 2 * ch] = value
            abuf[index, f, :, 2 * ch :] = jnp.where(
                final, 0.0, pltpu.roll(wider, width - 1, 0)
            ).astype(BF16)

    n_space = 2 * chips

    def edge(r, target):
        return pltpu.make_async_remote_copy(
            src_ref=tim.at[r],
            dst_ref=halo.at[1 - r],
            send_sem=hsend.at[r],
            recv_sem=hrecv.at[1 - r],
            device_id=(t, target),
            device_id_type=MESH,
        )

    @pl.when(t >= 2)
    def _():
        for h in range(2):
            passed(h, 0, t - 2).wait_recv()

    tacc[...] = tacc[...] + mm(hist[0].reshape(rows, ch), wtime[0])

    for r in range(2):
        @pl.when(t >= 1)
        def _(r=r):
            passed(r, 1, t - 1).wait_recv()

        row = (tacc[pl.ds(r * width, width), :] + mm(hist[1, r], wtime[1])).astype(BF16)
        tim[r] = row
        goes = (s > 0) if r == 0 else (s < n_space - 1)

        @pl.when(goes)
        def _(r=r):
            edge(r, s - 1 if r == 0 else s + 1).start()

        spread(1 + r, row)

    def convolve(j):
        upper, pr = ((0, 0), (1, 1), (1, 0), (2, 1))[j]
        for pc in range(2):
            value = jnp.concatenate([row_of(bspace, 0, c2), jnp.zeros((1, 256 - c2), F32)], axis=1)
            for dr in range(2):
                lhs = abuf[upper + dr, :, :, pc * ch : (pc + 2) * ch].reshape(rows, 2 * ch)
                value = value + mm_t(lhs, wf[pr, pc, :, 2 * dr * ch : 2 * (dr + 1) * ch])
            for half in range(2):
                for f in range(2):
                    wide[half, f, pl.ds(pc, width, stride=2), :] = value[
                        f * width : (f + 1) * width, half * 128 : (half + 1) * 128
                    ]
        for f in range(2):
            outv[j, f, :, :128] = wide[0, f].astype(BF16)
            outv[j, f, :, 128:] = wide[1, f, :, : c2 - 128].astype(BF16)

    def give(j):
        return pltpu.make_async_copy(outv.at[j], out_h.at[:, j], osem.at[j])

    for j in (1, 2):
        convolve(j)
        give(j).start()

    for side in range(2):
        comes = (s > 0) if side == 0 else (s < n_space - 1)

        @pl.when(comes)
        def _(side=side):
            edge(1 - side, s - 1 if side == 0 else s + 1).wait_recv()

        @pl.when(jnp.logical_not(comes))
        def _(side=side):
            halo[side] = jnp.zeros(halo.shape[1:], BF16)

        spread(3 * side, halo[side])
        convolve(3 * side)
        give(3 * side).start()

    for h in range(2):
        @pl.when(has_hi)
        def _(h=h):
            block(z, c, h, 0, s + 2).wait_send()

        @pl.when(has_lo)
        def _(h=h):
            block(z, c, h, 2, s - 2).wait_send()

        block(z, c, h, 1, sib).wait_send()

    @pl.loop(1, chips)
    def _(d):
        for h in range(2):
            for origin, there, onward, target in (
                (z - d, z - d >= 0, has_hi, s + 2),
                (z + d, z + d <= chips - 1, has_lo, s - 2),
            ):
                @pl.when(there)
                def _(origin=origin, onward=onward, target=target, h=h):
                    @pl.when(onward)
                    def _():
                        block(origin, c, h, 0, target).wait_send()

                    block(origin, c, h, 1, sib).wait_send()

    for h in range(2):
        @pl.when(t < steps - 1)
        def _(h=h):
            passed(h, 1, t + 1).wait_send()

        @pl.when(t < steps - 2)
        def _(h=h):
            passed(h, 0, t + 2).wait_send()

    @pl.when(s > 0)
    def _():
        edge(0, s - 1).wait_send()

    @pl.when(s < n_space - 1)
    def _():
        edge(1, s + 1).wait_send()

    for j in range(4):
        give(j).wait()


def handed_on(source, target, held, into, out):
    places = [(f, j) for f in range(2) for j in range(4)]
    comes = [
        pltpu.make_async_copy(source.at[f, j], held.at[f, j], into.at[f, j]) for f, j in places
    ]
    goes = [pltpu.make_async_copy(held.at[f, j], target.at[f, j], out.at[f, j]) for f, j in places]
    for come in comes:
        come.start()
    for come, go in zip(comes, goes):
        come.wait()
        go.start()
    for go in goes:
        go.wait()


def solution(mesh):
    chips, steps = mesh.shape["space"] // 2, mesh.shape["tm"]

    def body(frames, cache, gain, wqkv, bqkv, wproj, bproj, wtime, btime, wspace, bspace):
        _, _, width, ch = frames.shape
        c2 = wspace.shape[-1]
        wspace = jnp.swapaxes(wspace, 2, 3)
        cache = cache.reshape((2,) + frames.shape[1:])
        rows = 2 * width
        vmem = pl.BlockSpec(memory_space=pltpu.VMEM)
        away = pl.BlockSpec(memory_space=pl.ANY)
        dma = pltpu.SemaphoreType.DMA
        made = pl.pallas_call(
            functools.partial(kernel, chips, steps),
            out_shape=jax.ShapeDtypeStruct((2, 4, 2 * width, c2), BF16),
            in_specs=[vmem, away, vmem, away, vmem, away, vmem, away, vmem, away, vmem],
            out_specs=away,
            scratch_shapes=[
                pltpu.VMEM((chips, 2, rows, ch), BF16),
                pltpu.VMEM(wqkv.shape, BF16),
                pltpu.VMEM(wproj.shape, BF16),
                pltpu.VMEM(wtime.shape, BF16),
                pltpu.VMEM(wspace.shape, BF16),
                pltpu.VMEM((2, 2, 256, 4 * ch), BF16),
                pltpu.VMEM((rows, ch), BF16),
                pltpu.VMEM((rows, 1), F32),
                pltpu.VMEM((rows, 1), F32),
                pltpu.VMEM((rows, ch), F32),
                pltpu.VMEM((2, width, ch), BF16),
                pltpu.VMEM((2, 2, width, ch), BF16),
                pltpu.VMEM((rows, 2 * ch), F32),
                pltpu.VMEM((2, width, 2 * ch), BF16),
                pltpu.VMEM((2, width, 2 * ch), BF16),
                pltpu.VMEM((4, 2, width, 3 * ch), BF16),
                pltpu.VMEM((2, 2, 2 * width, 128), F32),
                pltpu.VMEM((4, 2, 2 * width, c2), BF16),
                dma((4,)),
                dma((chips, 2, 2)),
                dma((chips, 2, 3)),
                dma((2, 2)),
                dma((2, 2)),
                dma((2,)),
                dma((2,)),
                dma((4,)),
                dma((2,)),
            ],
            compiler_params=pltpu.CompilerParams(
                collective_id=0, has_side_effects=True, vmem_limit_bytes=56 * 2**20
            ),
            cost_estimate=pl.CostEstimate(
                flops=2 * 10**9, bytes_accessed=6 * 10**6, transcendentals=300000
            ),
        )(frames, cache, gain, wqkv, bqkv, wproj, bproj, wtime, btime, wspace, bspace)
        return pl.pallas_call(
            handed_on,
            out_shape=jax.ShapeDtypeStruct(made.shape, BF16),
            in_specs=[away],
            out_specs=away,
            scratch_shapes=[pltpu.VMEM(made.shape, BF16), dma((2, 4)), dma((2, 4))],
            compiler_params=pltpu.CompilerParams(vmem_limit_bytes=60 * 2**20),
        )(made)

    return jax.shard_map(
        body,
        mesh=mesh,
        in_specs=(P("tm", "space", None, None), P(None, "space", None, None)) + (P(),) * 9,
        out_specs=P("tm", "space", None, None),
        check_vma=False,
    )
```
